512 devices in a mesh: outer: 64 (over z_lo, y, core), inner: 8 (over z_hi, x).
Axes of the slice: x: 4, y: 8, z: 8 (z_hi: 2, z_lo: 4; z = z_hi * 4 + z_lo), core: 2. Of those that a mesh axis runs over, the one named last changes fastest.
Arguments:
- queries: bfloat16 [98304, 1024], P(('outer', 'inner')), may hold values from -8 to 8
- keys: bfloat16 [98304, 1024], P(('outer', 'inner')), may hold values from -6 to 6
- values: bfloat16 [98304, 1024], P(('outer', 'inner')), may hold values from -6 to 6
- d_out: bfloat16 [98304, 1024], P(('outer', 'inner')), may hold values from -6 to 6
Outputs:
- attended: bfloat16 [98304, 1024], P(('outer', 'inner'))
- d_queries: bfloat16 [98304, 1024], P(('outer', 'inner'))
- d_keys: bfloat16 [98304, 1024], P(('outer', 'inner'))
- d_values: bfloat16 [98304, 1024], P(('outer', 'inner'))
The draws below stay inside these ranges and needn't reach their ends.
All inputs are finite; a program needn't handle non-finite values.
Results may differ from the reference program's by a relative error of at most 0.01.
Values may be sent and summed in bfloat16 or wider, within the bound.
A program may use at most 64 MiB of HBM per device.

```python
import jax
import jax.numpy as jnp
from jax import lax

HEADS = 8
HEAD_DIM = 128
HOPS = 4
TOK_DEV = 192
TOKENS = 98304
N_OUTER = 64
N_INNER = 8


def draw_keys(key, part):
    key = jax.random.fold_in(key, 11)
    feat_width = HEADS * HEAD_DIM
    base = jnp.clip(1.5 * jax.random.normal(key, (TOKENS, feat_width), jnp.float32), -6.0, 6.0)
    return base.astype(jnp.bfloat16)


def draw_queries(key, part):
    key = jax.random.fold_in(key, 23)
    feat_width = HEADS * HEAD_DIM
    base = jnp.clip(1.5 * jax.random.normal(key, (TOKENS, feat_width), jnp.float32), -6.0, 6.0)
    return base.astype(jnp.bfloat16)


def steps_of(own_key, extent, cuts, least, top_value):
    def one(axis_at, shards_of):
        heights = jax.random.uniform(jax.random.fold_in(jax.random.fold_in(own_key, 6), axis_at), (shards_of,), jnp.float32, least / len(cuts), top_value / len(cuts))
        return jnp.repeat(jnp.exp(heights), extent[axis_at] // shards_of).reshape((-1,) + (1,) * (len(extent) - axis_at - 1))

    gain = one(*cuts[0])
    for cut in cuts[1:]:
        gain = gain * one(*cut)
    return gain


def centred(rng, extent, width, bound, split=(), kind=jnp.bfloat16):
    factor_of = steps_of(rng, extent, split, -0.22, 0.18) if split else 1.0
    array = jax.random.normal(rng, extent, jnp.float32) * width * factor_of
    return jnp.minimum(jnp.maximum(array, -bound), bound).astype(kind)


def setup_inputs(seed: int = 0) -> dict:
    key_of = jax.random.split(jax.random.key(seed), 5)
    return {
        "queries": draw_queries(jax.random.fold_in(key_of[4], 71), 0),
        "keys": draw_keys(jax.random.fold_in(key_of[4], 71), 0),
        "values": centred(key_of[2], (TOKENS, HEADS * HEAD_DIM), 1.0, 6.0, ((0, 512),)),
        "d_out": centred(key_of[3], (TOKENS, HEADS * HEAD_DIM), 1.0, 6.0, ((0, 512),)),
    }


def attend(query_blk, key_win, value_win, grad_blk, key_live):
    scale = HEAD_DIM ** -0.5
    q_heads = query_blk.astype(jnp.float32).reshape(query_blk.shape[0], HEADS, HEAD_DIM)
    k_heads = key_win.astype(jnp.float32).reshape(key_win.shape[0], HEADS, HEAD_DIM)
    v_heads = value_win.astype(jnp.float32).reshape(key_win.shape[0], HEADS, HEAD_DIM)
    g_heads = grad_blk.astype(jnp.float32).reshape(query_blk.shape[0], HEADS, HEAD_DIM)
    scores = jnp.einsum("qhd,khd->hqk", q_heads, k_heads) * scale
    scores = jnp.where(key_live[None, None, :], scores, -1e30)
    highest = jnp.max(scores, axis=-1, keepdims=True)
    expo = jnp.exp(scores - highest)
    attn_weight = expo / jnp.sum(expo, axis=-1, keepdims=True)
    weight_b = lax.optimization_barrier(attn_weight.astype(jnp.bfloat16)).astype(jnp.float32)
    attended = jnp.einsum("hqk,khd->qhd", weight_b, v_heads).astype(jnp.bfloat16)
    delta = jnp.sum(g_heads * attended.astype(jnp.float32), axis=-1)
    dprob = jnp.einsum("qhd,khd->hqk", g_heads, v_heads)
    dscore = attn_weight * (dprob - jnp.transpose(delta)[:, :, None])
    dscore_b = lax.optimization_barrier(dscore.astype(jnp.bfloat16)).astype(jnp.float32)
    d_query = (jnp.einsum("hqk,khd->qhd", dscore_b, k_heads) * scale).astype(jnp.bfloat16)
    part_v = jnp.einsum("hqk,qhd->khd", weight_b, g_heads).astype(jnp.bfloat16)
    part_k = (jnp.einsum("hqk,qhd->khd", dscore_b, q_heads) * scale).astype(jnp.bfloat16)
    row_count = query_blk.shape[0]
    feat_width = query_blk.shape[1]
    return (attended.reshape(row_count, feat_width), d_query.reshape(row_count, feat_width),
            part_k.reshape(-1, feat_width), part_v.reshape(-1, feat_width))


def reference(queries, keys, values, d_out):
    feat_width = HEADS * HEAD_DIM
    grid_shape = (N_OUTER, N_INNER, TOK_DEV, feat_width)
    q_grid = queries.reshape(grid_shape)
    k_grid = keys.reshape(grid_shape)
    v_grid = values.reshape(grid_shape)
    g_grid = d_out.reshape(grid_shape)
    hop_index = jnp.arange(HOPS, dtype=jnp.int32)

    def window(arr, outer_idx):
        pieces = []
        for hop in range(HOPS):
            source = jnp.maximum(outer_idx - hop, 0).astype(jnp.int32)
            block = lax.dynamic_index_in_dim(arr, source, 0, keepdims=False)
            pieces.append(jnp.stack([jnp.roll(block, 1, 0), block, jnp.roll(block, -1, 0)], 1))
        return jnp.stack(pieces, 1).reshape(N_INNER, HOPS * 3 * TOK_DEV, feat_width)

    def send_home(accum, parts, outer_idx, live_hops):
        for hop in range(HOPS):
            cols = parts[:, hop]
            gathered = jnp.roll(cols[:, 0], -1, 0) + cols[:, 1] + jnp.roll(cols[:, 2], 1, 0)
            gathered = jnp.where(live_hops[hop], gathered, jnp.float32(0.0))
            target = jnp.maximum(outer_idx - hop, 0).astype(jnp.int32)
            current = lax.dynamic_index_in_dim(accum, target, 0, keepdims=False)
            accum = lax.dynamic_update_index_in_dim(accum, current + gathered, target, 0)
        return accum

    def step(carry, outer_idx):
        acc_keys, acc_values = carry
        live_hops = (outer_idx - hop_index) >= 0
        key_live = jnp.broadcast_to(live_hops[:, None], (HOPS, 3 * TOK_DEV)).reshape(-1)
        q_blk = lax.dynamic_index_in_dim(q_grid, outer_idx, 0, keepdims=False)
        g_blk = lax.dynamic_index_in_dim(g_grid, outer_idx, 0, keepdims=False)
        k_win = window(k_grid, outer_idx)
        v_win = window(v_grid, outer_idx)
        attended, d_query, part_k, part_v = jax.vmap(attend, in_axes=(0, 0, 0, 0, None))(q_blk, k_win, v_win, g_blk, key_live)
        part_k = part_k.astype(jnp.float32).reshape(N_INNER, HOPS, 3, TOK_DEV, feat_width)
        part_v = part_v.astype(jnp.float32).reshape(N_INNER, HOPS, 3, TOK_DEV, feat_width)
        acc_keys = send_home(acc_keys, part_k, outer_idx, live_hops)
        acc_values = send_home(acc_values, part_v, outer_idx, live_hops)
        return (acc_keys, acc_values), (attended, d_query)

    zeros = jnp.zeros(grid_shape, jnp.float32)
    (acc_keys, acc_values), (attended, d_query) = lax.scan(step, (zeros, zeros), jnp.arange(N_OUTER, dtype=jnp.int32))
    full_shape = (TOKENS, feat_width)
    return (attended.reshape(full_shape), d_query.reshape(full_shape),
            acc_keys.astype(jnp.bfloat16).reshape(full_shape), acc_values.astype(jnp.bfloat16).reshape(full_shape))
```

```python
import jax
import jax.numpy as jnp
from jax import lax
from jax.experimental import pallas as pl
from jax.experimental.pallas import tpu as pltpu
from jax.sharding import PartitionSpec as P

HEADS = 8
DIM = 128
HOPS = 4
ROWS = 192
KEYS = 3 * ROWS
QUERIES = HOPS * ROWS
TILE = 256
SCALE = DIM ** (-0.5)
LOG2E = 1.4426950408889634
STAT_FROM = (-3, -2, -1, 1, 2, 3)
MESH = pl.DeviceIdType.MESH
F32 = jnp.float32
BF16 = jnp.bfloat16


def nt_dot(a, b):
    return lax.dot_general(a, b, (((1,), (1,)), ((), ())), preferred_element_type=F32)


def tn_dot(a, b):
    return lax.dot_general(a, b, (((0,), (0,)), ((), ())), preferred_element_type=F32)


def kernel(
    q_in, k_in, v_in, g_in,
    o_out, dq_out, dk_out, dv_out,
    kv, qg, prob, dprob, wb, ds, top, st_send, st_recv,
    own_kv, rk_send, rk_recv, oq, rq_recv,
    load_sem, kv_ss, kv_rs, qg_ss, qg_rs, st_ss, st_rs, rk_ss, rk_rs, rq_ss, rq_rs,
):
    o = lax.axis_index("outer")
    i = lax.axis_index("inner")
    n_outer = lax.axis_size("outer")
    n_inner = lax.axis_size("inner")
    left = lax.rem(i + n_inner - 1, n_inner)
    right = lax.rem(i + 1, n_inner)
    slot = lax.rem(o, HOPS)

    def exists(delta):
        return o + delta >= 0 if delta < 0 else o + delta < n_outer

    def load(n):
        cols = pl.ds(pl.multiple_of(n * DIM, DIM), DIM)
        return (
            pltpu.make_async_copy(k_in.at[:, cols], kv.at[n, 1, 0], load_sem.at[n, 0]),
            pltpu.make_async_copy(v_in.at[:, cols], kv.at[n, 1, 1], load_sem.at[n, 1]),
            pltpu.make_async_copy(q_in.at[:, cols], qg.at[n, slot, 0], load_sem.at[n, 2]),
            pltpu.make_async_copy(g_in.at[:, cols], qg.at[n, slot, 1], load_sem.at[n, 3]),
        )

    @pl.loop(0, HEADS)
    def _(n):
        for copy in load(n):
            copy.start()

    barrier = pltpu.get_barrier_semaphore()
    for other in (left, right):
        pl.semaphore_signal(barrier, inc=1, device_id=(o, other), device_id_type=MESH)
    for delta in STAT_FROM:
        @pl.when(exists(delta))
        def _():
            pl.semaphore_signal(barrier, inc=1, device_id=(o + delta, i), device_id_type=MESH)

    for h in range(1, HOPS):
        @pl.when(jnp.logical_not(exists(h)))
        def _():
            qg[:, lax.rem(o + h, HOPS)] = jnp.zeros((HEADS, 2, ROWS, DIM), BF16)

        @pl.when(jnp.logical_not(exists(-h)))
        def _():
            rq_recv[:, h - 1] = jnp.zeros((HEADS, 2, ROWS, DIM), BF16)
    for at, delta in enumerate(STAT_FROM):
        @pl.when(jnp.logical_not(exists(delta)))
        def _():
            st_recv[:, at] = jnp.zeros((HEADS, 2, QUERIES), F32)

    behind = jnp.minimum(o, HOPS - 1)
    ahead = jnp.minimum(n_outer - 1 - o, HOPS - 1)
    pl.semaphore_wait(barrier, 2 + behind + ahead)

    def kv_copy(n, to):
        return pltpu.make_async_remote_copy(
            kv.at[n, 1], kv.at[n, 2 - 2 * to], kv_ss.at[n, to], kv_rs.at[n, to],
            device_id=(o, (left, right)[to]), device_id_type=MESH,
        )

    def qg_copy(n, h):
        return pltpu.make_async_remote_copy(
            qg.at[n, slot], qg.at[n, slot], qg_ss.at[n, h - 1], qg_rs.at[n, h - 1],
            device_id=(o - h, i), device_id_type=MESH,
        )

    def qg_arrival(n, h):
        at = lax.rem(o + h, HOPS)
        return pltpu.make_async_remote_copy(
            qg.at[n, at], qg.at[n, at], qg_ss.at[n, h - 1], qg_rs.at[n, h - 1],
            device_id=(o, i), device_id_type=MESH,
        )

    def st_copy(n, delta):
        at = STAT_FROM.index(-delta)
        return pltpu.make_async_remote_copy(
            st_send.at[n], st_recv.at[n, at], st_ss.at[n, at], st_rs.at[n, at],
            device_id=(o + delta, i), device_id_type=MESH,
        )

    def rk_copy(n, to):
        return pltpu.make_async_remote_copy(
            rk_send.at[n, to], rk_recv.at[n, to], rk_ss.at[n, to], rk_rs.at[n, to],
            device_id=(o, (left, right)[to]), device_id_type=MESH,
        )

    def rq_copy(n, h):
        return pltpu.make_async_remote_copy(
            oq.at[n, lax.rem(o + h, HOPS)], rq_recv.at[n, h - 1],
            rq_ss.at[n, h - 1], rq_rs.at[n, h - 1],
            device_id=(o + h, i), device_id_type=MESH,
        )

    @pl.loop(0, HEADS)
    def _(n):
        for copy in load(n):
            copy.wait()
        for to in range(2):
            kv_copy(n, to).start()
        for h in range(1, HOPS):
            @pl.when(exists(-h))
            def _():
                qg_copy(n, h).start()

    lane = lax.broadcasted_iota(jnp.int32, (1, QUERIES), 1)
    at_slot = sum((lane >= ROWS * s).astype(jnp.int32) for s in range(1, HOPS))
    hop_of = (at_slot - slot + HOPS) & (HOPS - 1)

    def first(n):
        par = n & 1
        for to in range(2):
            kv_copy(n, to).wait_recv()
        for h in range(1, HOPS):
            @pl.when(exists(h))
            def _():
                qg_arrival(n, h).wait_recv()
        q = qg[n, :, 0].reshape(QUERIES, DIM)
        g = qg[n, :, 1].reshape(QUERIES, DIM)
        tops, sums, dots = [], [], []
        for b in range(3):
            k = kv[n, b, 0]
            v = kv[n, b, 1]
            t_row, s_row, d_row = [], [], []
            for t in range(QUERIES // TILE):
                cols = slice(t * TILE, (t + 1) * TILE)
                s = nt_dot(k, q[cols])
                high = jnp.max(s, axis=0, keepdims=True)
                p = jnp.exp2((s - high) * (SCALE * LOG2E))
                dp = nt_dot(v, g[cols])
                prob[par, b, :, cols] = p
                dprob[par, b, :, cols] = dp
                t_row.append(high * (SCALE * LOG2E))
                s_row.append(jnp.sum(p, axis=0, keepdims=True))
                d_row.append(jnp.sum(p * dp, axis=0, keepdims=True))
            tops.append(jnp.concatenate(t_row, axis=1))
            sums.append(jnp.concatenate(s_row, axis=1))
            dots.append(jnp.concatenate(d_row, axis=1))
            top[par, b] = tops[-1]
        best = jnp.maximum(jnp.maximum(tops[0], tops[1]), tops[2])
        total = jnp.zeros_like(best)
        dot = jnp.zeros_like(best)
        for b in range(3):
            factor = jnp.exp2(tops[b] - best)
            total += factor * sums[b]
            dot += factor * dots[b]
        st_send[n, 0:1, :] = best + jnp.log2(total)
        st_send[n, 1:2, :] = dot / total
        for delta in STAT_FROM:
            @pl.when(exists(delta))
            def _():
                st_copy(n, delta).start()

    def second(n):
        par = n & 1
        for delta in STAT_FROM:
            @pl.when(exists(delta))
            def _():
                st_copy(n, -delta).wait_recv()
        logs = [st_send[n, 0:1, :]]
        dots = [st_send[n, 1:2, :]]
        for at, delta in enumerate(STAT_FROM):
            shared = (hop_of >= delta) if delta > 0 else (hop_of <= HOPS - 1 + delta)
            shared = jnp.logical_and(shared, exists(delta))
            logs.append(jnp.where(shared, st_recv[n, at, 0:1, :], -1e30))
            dots.append(jnp.where(shared, st_recv[n, at, 1:2, :], 0.0))
        best = logs[0]
        for x in logs[1:]:
            best = jnp.maximum(best, x)
        total = jnp.zeros_like(best)
        delta_row = jnp.zeros_like(best)
        for x, d in zip(logs, dots):
            factor = jnp.exp2(x - best)
            total += factor
            delta_row += factor * d
        delta_row = delta_row / total
        log_all = best + jnp.log2(total)
        for b in range(3):
            factor = jnp.exp2(top[par, b] - log_all)
            w = prob[par, b] * factor
            wb[b] = w.astype(BF16)
            ds[b] = (w * (dprob[par, b] - delta_row)).astype(BF16)
        w_all = wb[...].reshape(KEYS, QUERIES)
        s_all = ds[...].reshape(KEYS, QUERIES)
        q = qg[n, :, 0].reshape(QUERIES, DIM)
        g = qg[n, :, 1].reshape(QUERIES, DIM)
        dv = jnp.dot(w_all, g, preferred_element_type=F32)
        dk = jnp.dot(s_all, q, preferred_element_type=F32) * SCALE
        for to, b in ((0, 0), (1, 2)):
            rk_send[n, to, 0] = dk[b * ROWS:(b + 1) * ROWS].astype(BF16)
            rk_send[n, to, 1] = dv[b * ROWS:(b + 1) * ROWS].astype(BF16)
            rk_copy(n, to).start()
        own_kv[n, 0] = dk[ROWS:2 * ROWS]
        own_kv[n, 1] = dv[ROWS:2 * ROWS]
        k_all = kv[n, :, 0].reshape(KEYS, DIM)
        v_all = kv[n, :, 1].reshape(KEYS, DIM)
        out = tn_dot(v_all, w_all).T
        dq = (tn_dot(k_all, s_all) * SCALE).T
        oq[n, :, 0] = out.astype(BF16).reshape(HOPS, ROWS, DIM)
        oq[n, :, 1] = dq.astype(BF16).reshape(HOPS, ROWS, DIM)
        for h in range(HOPS - 1, 0, -1):
            @pl.when(exists(h))
            def _():
                rq_copy(n, h).start()

    first(0)

    @pl.loop(1, HEADS)
    def _(n):
        first(n)
        second(n - 1)

    second(HEADS - 1)

    @pl.loop(0, HEADS)
    def _(n):
        for to in range(2):
            rk_copy(n, to).wait_recv()
        for h in range(1, HOPS):
            @pl.when(exists(-h))
            def _():
                rq_copy(n, h).wait_recv()
        cols = pl.ds(pl.multiple_of(n * DIM, DIM), DIM)
        for part, out in ((0, dk_out), (1, dv_out)):
            total = own_kv[n, part]
            for to in range(2):
                total += rk_recv[n, to, part].astype(F32)
            out[:, cols] = total.astype(BF16)
        for part, out in ((0, o_out), (1, dq_out)):
            total = oq[n, slot, part].astype(F32)
            for h in range(1, HOPS):
                total += rq_recv[n, h - 1, part].astype(F32)
            out[:, cols] = total.astype(BF16)

    @pl.loop(0, HEADS)
    def _(n):
        for to in range(2):
            kv_copy(n, to).wait_send()
            rk_copy(n, to).wait_send()
        for h in range(1, HOPS):
            @pl.when(exists(-h))
            def _():
                qg_copy(n, h).wait_send()

            @pl.when(exists(h))
            def _():
                rq_copy(n, h).wait_send()
        for delta in STAT_FROM:
            @pl.when(exists(delta))
            def _():
                st_copy(n, delta).wait_send()


def on_device(queries, keys, values, d_out):
    block = jax.ShapeDtypeStruct((ROWS, HEADS * DIM), BF16)
    vmem = pl.BlockSpec(memory_space=pltpu.VMEM)
    dma = pltpu.SemaphoreType.DMA
    return pl.pallas_call(
        kernel,
        out_shape=(block,) * 4,
        in_specs=[pl.BlockSpec(memory_space=pl.ANY)] * 4,
        out_specs=(vmem,) * 4,
        scratch_shapes=[
            pltpu.VMEM((HEADS, 3, 2, ROWS, DIM), BF16),
            pltpu.VMEM((HEADS, HOPS, 2, ROWS, DIM), BF16),
            pltpu.VMEM((2, 3, ROWS, QUERIES), F32),
            pltpu.VMEM((2, 3, ROWS, QUERIES), F32),
            pltpu.VMEM((3, ROWS, QUERIES), BF16),
            pltpu.VMEM((3, ROWS, QUERIES), BF16),
            pltpu.VMEM((2, 3, 1, QUERIES), F32),
            pltpu.VMEM((HEADS, 2, QUERIES), F32),
            pltpu.VMEM((HEADS, 6, 2, QUERIES), F32),
            pltpu.VMEM((HEADS, 2, ROWS, DIM), F32),
            pltpu.VMEM((HEADS, 2, 2, ROWS, DIM), BF16),
            pltpu.VMEM((HEADS, 2, 2, ROWS, DIM), BF16),
            pltpu.VMEM((HEADS, HOPS, 2, ROWS, DIM), BF16),
            pltpu.VMEM((HEADS, HOPS - 1, 2, ROWS, DIM), BF16),
            dma((HEADS, 4)),
            dma((HEADS, 2)), dma((HEADS, 2)),
            dma((HEADS, 3)), dma((HEADS, 3)),
            dma((HEADS, 6)), dma((HEADS, 6)),
            dma((HEADS, 2)), dma((HEADS, 2)),
            dma((HEADS, 3)), dma((HEADS, 3)),
        ],
        compiler_params=pltpu.CompilerParams(
            collective_id=0, has_side_effects=True, vmem_limit_bytes=56 << 20
        ),
        cost_estimate=pl.CostEstimate(
            flops=12 * HEADS * KEYS * QUERIES * DIM,
            bytes_accessed=8 * ROWS * HEADS * DIM * 2,
            transcendentals=HEADS * KEYS * QUERIES,
        ),
        name="window_attention",
    )(queries, keys, values, d_out)


def solution(mesh):
    placed = P(("outer", "inner"), None)
    return jax.shard_map(
        on_device,
        mesh=mesh,
        in_specs=(placed,) * 4,
        out_specs=(placed,) * 4,
        check_vma=False,
    )
```

```python
import jax
import jax.numpy as jnp
from jax import lax
from jax.experimental import pallas as pl
from jax.experimental.pallas import tpu as pltpu
from jax.sharding import PartitionSpec as P

HEADS = 8
DIM = 128
HOPS = 4
ROWS = 192
KEYS = 3 * ROWS
QUERIES = HOPS * ROWS
TILE = 256
SCALE = DIM ** (-0.5)
LOG2E = 1.4426950408889634
STAT_FROM = (-3, -2, -1, 1, 2, 3)
MESH = pl.DeviceIdType.MESH
F32 = jnp.float32
BF16 = jnp.bfloat16


def nt_dot(a, b):
    return lax.dot_general(a, b, (((1,), (1,)), ((), ())), preferred_element_type=F32)


def tn_dot(a, b):
    return lax.dot_general(a, b, (((0,), (0,)), ((), ())), preferred_element_type=F32)


def kernel(
    q_in, k_in, v_in, g_in,
    o_out, dq_out, dk_out, dv_out,
    kv, qg, prob, dprob, wb, ds, top, st_send, st_recv,
    own_kv, rk_send, rk_recv, relayed, oq, rq_recv,
    load_sem, kv_ss, kv_rs, kv_fs, qg_ss, qg_rs, st_ss, st_rs,
    rk_ss, rk_rs, re_ss, re_rs, rk_fs, rq_ss, rq_rs,
):
    o = lax.axis_index("outer")
    i = lax.axis_index("inner")
    n_outer = lax.axis_size("outer")
    n_inner = lax.axis_size("inner")
    left = lax.rem(i + n_inner - 1, n_inner)
    right = lax.rem(i + 1, n_inner)
    slot = lax.rem(o, HOPS)
    x = lax.rem(i, 4)
    first_x, last_x = x == 0, x == 3
    relays = jnp.logical_or(x == 1, x == 2)
    up = (x == 2).astype(jnp.int32)
    far = lax.rem(jnp.where(x >= 2, i + 2, i + n_inner - 2), n_inner)

    def exists(delta):
        return o + delta >= 0 if delta < 0 else o + delta < n_outer

    def load(n):
        cols = pl.ds(pl.multiple_of(n * DIM, DIM), DIM)
        return (
            pltpu.make_async_copy(k_in.at[:, cols], kv.at[n, 1, 0], load_sem.at[n, 0]),
            pltpu.make_async_copy(v_in.at[:, cols], kv.at[n, 1, 1], load_sem.at[n, 1]),
            pltpu.make_async_copy(q_in.at[:, cols], qg.at[n, slot, 0], load_sem.at[n, 2]),
            pltpu.make_async_copy(g_in.at[:, cols], qg.at[n, slot, 1], load_sem.at[n, 3]),
        )

    @pl.loop(0, HEADS)
    def _(n):
        for copy in load(n):
            copy.start()

    barrier = pltpu.get_barrier_semaphore()
    for other in (left, right, far):
        pl.semaphore_signal(barrier, inc=1, device_id=(o, other), device_id_type=MESH)
    for delta in STAT_FROM:
        @pl.when(exists(delta))
        def _():
            pl.semaphore_signal(barrier, inc=1, device_id=(o + delta, i), device_id_type=MESH)

    for h in range(1, HOPS):
        @pl.when(jnp.logical_not(exists(h)))
        def _():
            qg[:, lax.rem(o + h, HOPS)] = jnp.zeros((HEADS, 2, ROWS, DIM), BF16)
    for at, delta in enumerate(STAT_FROM):
        @pl.when(jnp.logical_not(exists(delta)))
        def _():
            st_recv[:, at] = jnp.zeros((HEADS, 2, QUERIES), F32)

    @pl.when(o == 0)
    def _():
        rq_recv[:, 0] = jnp.zeros((HEADS, 2, ROWS, DIM), BF16)

    behind = jnp.minimum(o, HOPS - 1)
    ahead = jnp.minimum(n_outer - 1 - o, HOPS - 1)
    pl.semaphore_wait(barrier, 3 + behind + ahead)

    def kv_copy(n, to):
        return pltpu.make_async_remote_copy(
            kv.at[n, 1], kv.at[n, 2 - 2 * to], kv_ss.at[n, to], kv_rs.at[n, to],
            device_id=(o, (left, right)[to]), device_id_type=MESH,
        )

    def relayed_to(n, to):
        return jnp.logical_and((first_x, last_x)[to], (n & 1) == 1)

    def kv_send(n):
        for to in range(2):
            @pl.when(jnp.logical_not(relayed_to(n, to)))
            def _():
                kv_copy(n, to).start()

    def kv_forward_copy(n):
        return pltpu.make_async_remote_copy(
            kv.at[n, 2 * up], kv.at[n, 2 - 2 * up], kv_fs.at[n >> 1], kv_rs.at[n, up],
            device_id=(o, far), device_id_type=MESH,
        )

    def kv_forward(n):
        @pl.when(x == 1)
        def _():
            kv_copy(n, 1).wait_recv()

        @pl.when(x == 2)
        def _():
            kv_copy(n, 0).wait_recv()

        @pl.when(relays)
        def _():
            kv_forward_copy(n).start()

    def kv_wait(n):
        odd = (n & 1) == 1
        for to in range(2):
            @pl.when(jnp.logical_not(jnp.logical_and(x == 2 - to, odd)))
            def _():
                kv_copy(n, to).wait_recv()

    def qg_copy(n, h):
        at = lax.rem(o + h, HOPS)
        return pltpu.make_async_remote_copy(
            qg.at[n, at], qg.at[n, at], qg_ss.at[n, h], qg_rs.at[n, h],
            device_id=(o - 1, i), device_id_type=MESH,
        )

    def qg_send(n, h):
        @pl.when(jnp.logical_and(o > 0, exists(h)))
        def _():
            qg_copy(n, h).start()

    def qg_wait(n, h):
        at = lax.rem(o + h, HOPS)

        @pl.when(exists(h))
        def _():
            pltpu.make_async_remote_copy(
                qg.at[n, at], qg.at[n, at], qg_ss.at[n, h - 1], qg_rs.at[n, h - 1],
                device_id=(o - 1, i), device_id_type=MESH,
            ).wait_recv()

    def qg_forward(n, h):
        qg_wait(n, h)
        qg_send(n, h)

    def st_copy(n, delta):
        at = STAT_FROM.index(-delta)
        return pltpu.make_async_remote_copy(
            st_send.at[n], st_recv.at[n, at], st_ss.at[n, at], st_rs.at[n, at],
            device_id=(o + delta, i), device_id_type=MESH,
        )

    def rk_copy(n, to):
        return pltpu.make_async_remote_copy(
            rk_send.at[n, to], rk_recv.at[n, to], rk_ss.at[n, to], rk_rs.at[n, to],
            device_id=(o, (left, right)[to]), device_id_type=MESH,
        )

    def relay_copy(n, to):
        return pltpu.make_async_remote_copy(
            rk_send.at[n, to], relayed.at[n >> 1], re_ss.at[n >> 1], re_rs.at[n >> 1],
            device_id=(o, (right, left)[to]), device_id_type=MESH,
        )

    def rk_start(n):
        for to in range(2):
            @pl.when(jnp.logical_not(relayed_to(n, to)))
            def _():
                rk_copy(n, to).start()

            @pl.when(relayed_to(n, to))
            def _():
                relay_copy(n, to).start()

    def rk_forward_copy(n):
        return pltpu.make_async_remote_copy(
            relayed.at[n >> 1], rk_recv.at[n, up], rk_fs.at[n >> 1], rk_rs.at[n, up],
            device_id=(o, far), device_id_type=MESH,
        )

    def rk_forward(n):
        @pl.when(relays)
        def _():
            relay_copy(n, 0).wait_recv()
            rk_forward_copy(n).start()

    def rq_copy(n, h):
        return pltpu.make_async_remote_copy(
            oq.at[n, lax.rem(o + h, HOPS)], rq_recv.at[n, h - 1],
            rq_ss.at[n, h - 1], rq_rs.at[n, h - 1],
            device_id=(o + 1, i), device_id_type=MESH,
        )

    def rq_send(n, h):
        @pl.when(exists(h))
        def _():
            rq_copy(n, h).start()

    def rq_wait(n, h):
        pltpu.make_async_remote_copy(
            oq.at[n, 0], rq_recv.at[n, h], rq_ss.at[n, h], rq_rs.at[n, h],
            device_id=(o + 1, i), device_id_type=MESH,
        ).wait_recv()

    def rq_pass(n, h):
        at = lax.rem(o + h, HOPS)

        @pl.when(jnp.logical_and(o > 0, exists(h)))
        def _():
            rq_wait(n, h)
            oq[n, at] = (oq[n, at].astype(F32) + rq_recv[n, h].astype(F32)).astype(BF16)

        rq_send(n, h)

    for n in range(HEADS):
        for copy in load(n):
            copy.wait()
        kv_send(n)
        qg_send(n, 0)

    lane = lax.broadcasted_iota(jnp.int32, (1, QUERIES), 1)
    at_slot = sum((lane >= ROWS * s).astype(jnp.int32) for s in range(1, HOPS))
    hop_of = (at_slot - slot + HOPS) & (HOPS - 1)

    def first(n):
        par = n & 1
        kv_wait(n)
        qg_wait(n, 3)
        q = qg[n, :, 0].reshape(QUERIES, DIM)
        g = qg[n, :, 1].reshape(QUERIES, DIM)
        tops, sums, dots = [], [], []
        for b in range(3):
            k = kv[n, b, 0]
            v = kv[n, b, 1]
            t_row, s_row, d_row = [], [], []
            for t in range(QUERIES // TILE):
                cols = slice(t * TILE, (t + 1) * TILE)
                s = nt_dot(k, q[cols])
                high = jnp.max(s, axis=0, keepdims=True)
                p = jnp.exp2((s - high) * (SCALE * LOG2E))
                dp = nt_dot(v, g[cols])
                prob[par, b, :, cols] = p
                dprob[par, b, :, cols] = dp
                t_row.append(high * (SCALE * LOG2E))
                s_row.append(jnp.sum(p, axis=0, keepdims=True))
                d_row.append(jnp.sum(p * dp, axis=0, keepdims=True))
            tops.append(jnp.concatenate(t_row, axis=1))
            sums.append(jnp.concatenate(s_row, axis=1))
            dots.append(jnp.concatenate(d_row, axis=1))
            top[par, b] = tops[-1]
        best = jnp.maximum(jnp.maximum(tops[0], tops[1]), tops[2])
        total = jnp.zeros_like(best)
        dot = jnp.zeros_like(best)
        for b in range(3):
            factor = jnp.exp2(tops[b] - best)
            total += factor * sums[b]
            dot += factor * dots[b]
        st_send[n, 0:1, :] = best + jnp.log2(total)
        st_send[n, 1:2, :] = dot / total
        for delta in STAT_FROM:
            @pl.when(exists(delta))
            def _():
                st_copy(n, delta).start()

    def second(n):
        par = n & 1
        for delta in STAT_FROM:
            @pl.when(exists(delta))
            def _():
                st_copy(n, -delta).wait_recv()
        logs = [st_send[n, 0:1, :]]
        dots = [st_send[n, 1:2, :]]
        for at, delta in enumerate(STAT_FROM):
            shared = (hop_of >= delta) if delta > 0 else (hop_of <= HOPS - 1 + delta)
            shared = jnp.logical_and(shared, exists(delta))
            logs.append(jnp.where(shared, st_recv[n, at, 0:1, :], -1e30))
            dots.append(jnp.where(shared, st_recv[n, at, 1:2, :], 0.0))
        best = logs[0]
        for x in logs[1:]:
            best = jnp.maximum(best, x)
        total = jnp.zeros_like(best)
        delta_row = jnp.zeros_like(best)
        for x, d in zip(logs, dots):
            factor = jnp.exp2(x - best)
            total += factor
            delta_row += factor * d
        delta_row = delta_row / total
        log_all = best + jnp.log2(total)
        for b in range(3):
            factor = jnp.exp2(top[par, b] - log_all)
            w = prob[par, b] * factor
            wb[b] = w.astype(BF16)
            ds[b] = (w * (dprob[par, b] - delta_row)).astype(BF16)
        w_all = wb[...].reshape(KEYS, QUERIES)
        s_all = ds[...].reshape(KEYS, QUERIES)
        q = qg[n, :, 0].reshape(QUERIES, DIM)
        g = qg[n, :, 1].reshape(QUERIES, DIM)
        dv = jnp.dot(w_all, g, preferred_element_type=F32)
        dk = jnp.dot(s_all, q, preferred_element_type=F32) * SCALE
        for to, b in ((0, 0), (1, 2)):
            rk_send[n, to, 0] = dk[b * ROWS:(b + 1) * ROWS].astype(BF16)
            rk_send[n, to, 1] = dv[b * ROWS:(b + 1) * ROWS].astype(BF16)
        rk_start(n)
        own_kv[n, 0] = dk[ROWS:2 * ROWS]
        own_kv[n, 1] = dv[ROWS:2 * ROWS]
        k_all = kv[n, :, 0].reshape(KEYS, DIM)
        v_all = kv[n, :, 1].reshape(KEYS, DIM)
        out = tn_dot(v_all, w_all).T
        dq = (tn_dot(k_all, s_all) * SCALE).T
        oq[n, :, 0] = out.astype(BF16).reshape(HOPS, ROWS, DIM)
        oq[n, :, 1] = dq.astype(BF16).reshape(HOPS, ROWS, DIM)
        rq_send(n, 3)

    def when_head(n, do, *rest):
        @pl.when(jnp.logical_and(n >= 0, n < HEADS))
        def _():
            do(n, *rest)

    def ahead_of(t):
        when_head(2 * t + 1, kv_forward)
        when_head(t + 2, qg_forward, 1)
        when_head(t + 1, qg_forward, 2)

    qg_forward(0, 1)
    qg_forward(1, 1)
    qg_forward(0, 2)
    ahead_of(0)
    first(0)

    @pl.loop(1, HEADS)
    def _(t):
        ahead_of(t)
        first(t)
        second(t - 1)
        when_head(t - 2, rq_pass, 2)
        when_head(t - 3, rq_pass, 1)

        @pl.when(jnp.logical_and(t >= 3, (t & 1) == 1))
        def _():
            rk_forward(t - 2)

    second(HEADS - 1)
    rq_pass(HEADS - 2, 2)
    rq_pass(HEADS - 3, 1)
    rq_pass(HEADS - 1, 2)
    rq_pass(HEADS - 2, 1)
    rq_pass(HEADS - 1, 1)
    rk_forward(HEADS - 1)

    @pl.loop(0, HEADS)
    def _(n):
        for to in range(2):
            rk_copy(n, to).wait_recv()

        @pl.when(o > 0)
        def _():
            rq_wait(n, 0)

        cols = pl.ds(pl.multiple_of(n * DIM, DIM), DIM)
        for part, out in ((0, dk_out), (1, dv_out)):
            total = own_kv[n, part]
            for to in range(2):
                total += rk_recv[n, to, part].astype(F32)
            out[:, cols] = total.astype(BF16)
        for part, out in ((0, o_out), (1, dq_out)):
            out[:, cols] = (oq[n, slot, part].astype(F32) + rq_recv[n, 0, part].astype(F32)).astype(BF16)

    @pl.loop(0, HEADS)
    def _(n):
        for to in range(2):
            @pl.when(jnp.logical_not(relayed_to(n, to)))
            def _():
                kv_copy(n, to).wait_send()
                rk_copy(n, to).wait_send()

            @pl.when(relayed_to(n, to))
            def _():
                relay_copy(n, to).wait_send()

        @pl.when(jnp.logical_and(relays, (n & 1) == 1))
        def _():
            kv_forward_copy(n).wait_send()
            rk_forward_copy(n).wait_send()

        for h in range(HOPS - 1):
            @pl.when(jnp.logical_and(o > 0, exists(h)))
            def _():
                qg_copy(n, h).wait_send()

            @pl.when(exists(h + 1))
            def _():
                rq_copy(n, h + 1).wait_send()
        for delta in STAT_FROM:
            @pl.when(exists(delta))
            def _():
                st_copy(n, delta).wait_send()


def store(*refs):
    for a, b in zip(refs[:4], refs[4:]):
        b[...] = a[...]


def on_device(queries, keys, values, d_out):
    block = jax.ShapeDtypeStruct((ROWS, HEADS * DIM), BF16)
    vmem = pl.BlockSpec(memory_space=pltpu.VMEM)
    dma = pltpu.SemaphoreType.DMA
    results = pl.pallas_call(
        kernel,
        out_shape=(block,) * 4,
        in_specs=[pl.BlockSpec(memory_space=pl.ANY)] * 4,
        out_specs=(vmem,) * 4,
        scratch_shapes=[
            pltpu.VMEM((HEADS, 3, 2, ROWS, DIM), BF16),
            pltpu.VMEM((HEADS, HOPS, 2, ROWS, DIM), BF16),
            pltpu.VMEM((2, 3, ROWS, QUERIES), F32),
            pltpu.VMEM((2, 3, ROWS, QUERIES), F32),
            pltpu.VMEM((3, ROWS, QUERIES), BF16),
            pltpu.VMEM((3, ROWS, QUERIES), BF16),
            pltpu.VMEM((2, 3, 1, QUERIES), F32),
            pltpu.VMEM((HEADS, 2, QUERIES), F32),
            pltpu.VMEM((HEADS, 6, 2, QUERIES), F32),
            pltpu.VMEM((HEADS, 2, ROWS, DIM), F32),
            pltpu.VMEM((HEADS, 2, 2, ROWS, DIM), BF16),
            pltpu.VMEM((HEADS, 2, 2, ROWS, DIM), BF16),
            pltpu.VMEM((HEADS // 2, 2, ROWS, DIM), BF16),
            pltpu.VMEM((HEADS, HOPS, 2, ROWS, DIM), BF16),
            pltpu.VMEM((HEADS, HOPS - 1, 2, ROWS, DIM), BF16),
            dma((HEADS, 4)),
            dma((HEADS, 2)), dma((HEADS, 2)), dma((HEADS // 2,)),
            dma((HEADS, 3)), dma((HEADS, 3)),
            dma((HEADS, 6)), dma((HEADS, 6)),
            dma((HEADS, 2)), dma((HEADS, 2)),
            dma((HEADS // 2,)), dma((HEADS // 2,)), dma((HEADS // 2,)),
            dma((HEADS, 3)), dma((HEADS, 3)),
        ],
        compiler_params=pltpu.CompilerParams(
            collective_id=0, has_side_effects=True, vmem_limit_bytes=56 << 20
        ),
        cost_estimate=pl.CostEstimate(
            flops=12 * HEADS * KEYS * QUERIES * DIM,
            bytes_accessed=8 * ROWS * HEADS * DIM * 2,
            transcendentals=HEADS * KEYS * QUERIES,
        ),
        name="window_attention",
    )(queries, keys, values, d_out)
    return pl.pallas_call(
        store,
        out_shape=(block,) * 4,
        in_specs=[vmem] * 4,
        out_specs=(vmem,) * 4,
        name="store_results",
    )(*results)


def solution(mesh):
    placed = P(("outer", "inner"), None)
    return jax.shard_map(
        on_device,
        mesh=mesh,
        in_specs=(placed,) * 4,
        out_specs=(placed,) * 4,
        check_vma=False,
    )
```

```python
import jax
import jax.numpy as jnp
from jax import lax
from jax.experimental import pallas as pl
from jax.experimental.pallas import tpu as pltpu
from jax.sharding import PartitionSpec as P

HEADS = 8
DIM = 128
HOPS = 4
ROWS = 192
KEYS = 3 * ROWS
QUERIES = HOPS * ROWS
TILE = 256
SCALE = DIM ** (-0.5)
LOG2E = 1.4426950408889634
RUN = 16
LAG = 2
STAT_FROM = (-3, -2, -1, 1, 2, 3)
MESH = pl.DeviceIdType.MESH
F32 = jnp.float32
BF16 = jnp.bfloat16


def nt_dot(a, b):
    return lax.dot_general(a, b, (((1,), (1,)), ((), ())), preferred_element_type=F32)


def tn_dot(a, b):
    return lax.dot_general(a, b, (((0,), (0,)), ((), ())), preferred_element_type=F32)


def kernel(
    q_in, k_in, v_in, g_in,
    o_out, dq_out, dk_out, dv_out,
    kv, qg, prob, dprob, wb, ds, top, st_send, st_recv,
    own_kv, rk_send, rk_recv, relayed, oq, rq_recv, q_held, r_held,
    load_sem, kv_ss, kv_rs, kv_fs, qg_ss, qg_rs, qg_xs, ql_rs, ql_fs, st_ss, st_rs,
    rk_ss, rk_rs, re_ss, re_rs, rk_fs, rq_ss, rq_rs, rl_rs, rl_fs,
):
    o = lax.axis_index("outer")
    i = lax.axis_index("inner")
    n_outer = lax.axis_size("outer")
    n_inner = lax.axis_size("inner")
    left = lax.rem(i + n_inner - 1, n_inner)
    right = lax.rem(i + 1, n_inner)
    slot = lax.rem(o, HOPS)
    place = lax.rem(o, RUN)
    early, last = place <= HOPS - 2, place == RUN - 1
    run_before, run_after = o >= RUN, o < n_outer - RUN
    ends = jnp.logical_or(early, last)
    x = lax.rem(i, 4)
    first_x, last_x = x == 0, x == 3
    relays = jnp.logical_or(x == 1, x == 2)
    up = (x == 2).astype(jnp.int32)
    far = lax.rem(jnp.where(x >= 2, i + 2, i + n_inner - 2), n_inner)

    def exists(delta):
        return o + delta >= 0 if delta < 0 else o + delta < n_outer

    def load(n):
        cols = pl.ds(pl.multiple_of(n * DIM, DIM), DIM)
        return (
            pltpu.make_async_copy(k_in.at[:, cols], kv.at[n, 1, 0], load_sem.at[n, 0]),
            pltpu.make_async_copy(v_in.at[:, cols], kv.at[n, 1, 1], load_sem.at[n, 1]),
            pltpu.make_async_copy(q_in.at[:, cols], qg.at[n, slot, 0], load_sem.at[n, 2]),
            pltpu.make_async_copy(g_in.at[:, cols], qg.at[n, slot, 1], load_sem.at[n, 3]),
        )

    @pl.loop(0, HEADS)
    def _(n):
        for copy in load(n):
            copy.start()

    barrier = pltpu.get_barrier_semaphore()
    for other in (left, right, far):
        pl.semaphore_signal(barrier, inc=1, device_id=(o, other), device_id_type=MESH)
    for delta in STAT_FROM:
        @pl.when(exists(delta))
        def _():
            pl.semaphore_signal(barrier, inc=1, device_id=(o + delta, i), device_id_type=MESH)

    @pl.when(jnp.logical_and(ends, run_before))
    def _():
        pl.semaphore_signal(barrier, inc=1, device_id=(o - RUN, i), device_id_type=MESH)

    @pl.when(jnp.logical_and(ends, run_after))
    def _():
        pl.semaphore_signal(barrier, inc=1, device_id=(o + RUN, i), device_id_type=MESH)

    @pl.when(early)
    def _():
        pl.semaphore_signal(barrier, inc=1, device_id=(o + RUN - 1 - place, i), device_id_type=MESH)

    @pl.when(last)
    def _():
        for p in range(HOPS - 1):
            pl.semaphore_signal(barrier, inc=1, device_id=(o - RUN + 1 + p, i), device_id_type=MESH)

    for h in range(1, HOPS):
        @pl.when(jnp.logical_not(exists(h)))
        def _():
            qg[:, lax.rem(o + h, HOPS)] = jnp.zeros((HEADS, 2, ROWS, DIM), BF16)
    for at, delta in enumerate(STAT_FROM):
        @pl.when(jnp.logical_not(exists(delta)))
        def _():
            st_recv[:, at] = jnp.zeros((HEADS, 2, QUERIES), F32)

    @pl.when(o == 0)
    def _():
        rq_recv[:, 0] = jnp.zeros((HEADS, 2, ROWS, DIM), BF16)

    behind = jnp.minimum(o, HOPS - 1)
    ahead = jnp.minimum(n_outer - 1 - o, HOPS - 1)
    across = run_before.astype(jnp.int32) + run_after.astype(jnp.int32)
    more = jnp.where(early, 1 + across, jnp.where(last, HOPS - 1 + across, 0))
    pl.semaphore_wait(barrier, 3 + behind + ahead + more)

    def kv_copy(n, to):
        return pltpu.make_async_remote_copy(
            kv.at[n, 1], kv.at[n, 2 - 2 * to], kv_ss.at[n, to], kv_rs.at[n, to],
            device_id=(o, (left, right)[to]), device_id_type=MESH,
        )

    def relayed_to(n, to):
        return jnp.logical_and((first_x, last_x)[to], (n & 1) == 1)

    def kv_send(n):
        for to in range(2):
            @pl.when(jnp.logical_not(relayed_to(n, to)))
            def _():
                kv_copy(n, to).start()

    def kv_forward_copy(n):
        return pltpu.make_async_remote_copy(
            kv.at[n, 2 * up], kv.at[n, 2 - 2 * up], kv_fs.at[n >> 1], kv_rs.at[n, up],
            device_id=(o, far), device_id_type=MESH,
        )

    def kv_forward(n):
        @pl.when(x == 1)
        def _():
            kv_copy(n, 1).wait_recv()

        @pl.when(x == 2)
        def _():
            kv_copy(n, 0).wait_recv()

        @pl.when(relays)
        def _():
            kv_forward_copy(n).start()

    def kv_wait(n):
        odd = (n & 1) == 1
        for to in range(2):
            @pl.when(jnp.logical_not(jnp.logical_and(x == 2 - to, odd)))
            def _():
                kv_copy(n, to).wait_recv()

    def qg_copy(n, h):
        at = lax.rem(o + h, HOPS)
        return pltpu.make_async_remote_copy(
            qg.at[n, at], qg.at[n, at], qg_ss.at[n, h], qg_rs.at[n, h],
            device_id=(o - 1, i), device_id_type=MESH,
        )

    def qg_turns(n):
        return jnp.logical_or(place == 2, jnp.logical_and(place < 2, (n & 1) == 1))

    def qg_relayed(n):
        return jnp.logical_and(run_before, qg_turns(n))

    def qg_sends(n, h):
        here = jnp.logical_and(o > 0, exists(h))
        if h == 0:
            return jnp.logical_and(here, jnp.logical_not(jnp.logical_and(place == 0, qg_relayed(n))))
        return jnp.logical_and(here, place > 0)

    def qg_cross_copy(n, h):
        return pltpu.make_async_remote_copy(
            qg.at[n, slot], qg.at[n, slot], qg_xs.at[n], qg_rs.at[n, h - 1],
            device_id=(o - h, i), device_id_type=MESH,
        )

    def qg_crosses(n, h):
        here = jnp.logical_and(run_before, place == h - 1)
        return jnp.logical_and(here, jnp.logical_not(qg_turns(n)))

    def qg_relay_copy(n):
        return pltpu.make_async_remote_copy(
            qg.at[n, slot], q_held.at[n], qg_xs.at[n], ql_rs.at[n],
            device_id=(o - RUN, i), device_id_type=MESH,
        )

    def qg_pass_copy(n):
        return pltpu.make_async_remote_copy(
            q_held.at[n], qg.at[n, slot], ql_fs.at[n], qg_rs.at[n, place],
            device_id=(o + RUN - 1 - place, i), device_id_type=MESH,
        )

    def qg_passes(n):
        return jnp.logical_and(run_after, qg_turns(n))

    def qg_pass(n):
        @pl.when(qg_passes(n))
        def _():
            qg_relay_copy(n).wait_recv()
            qg_pass_copy(n).start()

    def qg_send(n, h):
        @pl.when(qg_sends(n, h))
        def _():
            qg_copy(n, h).start()

        if h == 0:
            @pl.when(qg_crosses(n, 2))
            def _():
                qg_cross_copy(n, 2).start()

            @pl.when(qg_relayed(n))
            def _():
                qg_relay_copy(n).start()

    def qg_wait(n, h):
        at = lax.rem(o + h, HOPS)

        @pl.when(exists(h))
        def _():
            pltpu.make_async_remote_copy(
                qg.at[n, at], qg.at[n, at], qg_ss.at[n, h - 1], qg_rs.at[n, h - 1],
                device_id=(o - 1, i), device_id_type=MESH,
            ).wait_recv()

    def qg_forward(n, h):
        qg_wait(n, h)
        qg_send(n, h)

    def st_copy(n, delta):
        at = STAT_FROM.index(-delta)
        return pltpu.make_async_remote_copy(
            st_send.at[n], st_recv.at[n, at], st_ss.at[n, at], st_rs.at[n, at],
            device_id=(o + delta, i), device_id_type=MESH,
        )

    def rk_copy(n, to):
        return pltpu.make_async_remote_copy(
            rk_send.at[n, to], rk_recv.at[n, to], rk_ss.at[n, to], rk_rs.at[n, to],
            device_id=(o, (left, right)[to]), device_id_type=MESH,
        )

    def relay_copy(n, to):
        return pltpu.make_async_remote_copy(
            rk_send.at[n, to], relayed.at[n >> 1], re_ss.at[n >> 1], re_rs.at[n >> 1],
            device_id=(o, (right, left)[to]), device_id_type=MESH,
        )

    def rk_start(n):
        for to in range(2):
            @pl.when(jnp.logical_not(relayed_to(n, to)))
            def _():
                rk_copy(n, to).start()

            @pl.when(relayed_to(n, to))
            def _():
                relay_copy(n, to).start()

    def rk_forward_copy(n):
        return pltpu.make_async_remote_copy(
            relayed.at[n >> 1], rk_recv.at[n, up], rk_fs.at[n >> 1], rk_rs.at[n, up],
            device_id=(o, far), device_id_type=MESH,
        )

    def rk_forward(n):
        @pl.when(relays)
        def _():
            relay_copy(n, 0).wait_recv()
            rk_forward_copy(n).start()

    def rq_copy(n, h):
        return pltpu.make_async_remote_copy(
            oq.at[n, lax.rem(o + h, HOPS)], rq_recv.at[n, h - 1],
            rq_ss.at[n, h - 1], rq_rs.at[n, h - 1],
            device_id=(o + 1, i), device_id_type=MESH,
        )

    def rq_relay_copy(n, h):
        return pltpu.make_async_remote_copy(
            oq.at[n, lax.rem(o + h, HOPS)], r_held.at[n >> 1, h - 1],
            rq_ss.at[n, h - 1], rl_rs.at[n >> 1, h - 1],
            device_id=(o + RUN, i), device_id_type=MESH,
        )

    def rq_over_copy(n, h):
        return pltpu.make_async_remote_copy(
            r_held.at[n >> 1, h - 1], rq_recv.at[n, h - 1],
            rl_fs.at[n >> 1, h - 1], rq_rs.at[n, h - 1],
            device_id=(o - RUN + 1, i), device_id_type=MESH,
        )

    rq_passes = jnp.logical_and(last, run_before)

    def rq_over(n, h):
        @pl.when(rq_passes)
        def _():
            rq_relay_copy(n, h).wait_recv()
            rq_over_copy(n, h).start()

    def rq_relayed(n):
        return jnp.logical_and(last, (n & 1) == 1)

    def rq_send(n, h):
        @pl.when(jnp.logical_and(exists(h), rq_relayed(n)))
        def _():
            rq_relay_copy(n, h).start()

        @pl.when(jnp.logical_and(exists(h), jnp.logical_not(rq_relayed(n))))
        def _():
            rq_copy(n, h).start()

    def rq_wait(n, h):
        pltpu.make_async_remote_copy(
            oq.at[n, 0], rq_recv.at[n, h], rq_ss.at[n, h], rq_rs.at[n, h],
            device_id=(o + 1, i), device_id_type=MESH,
        ).wait_recv()

    def rq_pass(n, h):
        at = lax.rem(o + h, HOPS)

        @pl.when(jnp.logical_and(o > 0, exists(h)))
        def _():
            rq_wait(n, h)
            oq[n, at] = (oq[n, at].astype(F32) + rq_recv[n, h].astype(F32)).astype(BF16)

        rq_send(n, h)

    for n in range(HEADS):
        for copy in load(n):
            copy.wait()
        if n < 4:
            kv_send(n)
            qg_send(n, 0)

    lane = lax.broadcasted_iota(jnp.int32, (1, QUERIES), 1)
    at_slot = sum((lane >= ROWS * s).astype(jnp.int32) for s in range(1, HOPS))
    hop_of = (at_slot - slot + HOPS) & (HOPS - 1)

    def first(n):
        par = lax.rem(n, LAG + 1)
        kv_wait(n)
        qg_wait(n, 3)
        q = qg[n, :, 0].reshape(QUERIES, DIM)
        g = qg[n, :, 1].reshape(QUERIES, DIM)
        tops, sums, dots = [], [], []
        for b in range(3):
            k = kv[n, b, 0]
            v = kv[n, b, 1]
            t_row, s_row, d_row = [], [], []
            for t in range(QUERIES // TILE):
                cols = slice(t * TILE, (t + 1) * TILE)
                s = nt_dot(k, q[cols])
                high = jnp.max(s, axis=0, keepdims=True)
                p = jnp.exp2((s - high) * (SCALE * LOG2E))
                dp = nt_dot(v, g[cols])
                prob[par, b, :, cols] = p
                dprob[par, b, :, cols] = dp
                t_row.append(high * (SCALE * LOG2E))
                s_row.append(jnp.sum(p, axis=0, keepdims=True))
                d_row.append(jnp.sum(p * dp, axis=0, keepdims=True))
            tops.append(jnp.concatenate(t_row, axis=1))
            sums.append(jnp.concatenate(s_row, axis=1))
            dots.append(jnp.concatenate(d_row, axis=1))
            top[par, b] = tops[-1]
        best = jnp.maximum(jnp.maximum(tops[0], tops[1]), tops[2])
        total = jnp.zeros_like(best)
        dot = jnp.zeros_like(best)
        for b in range(3):
            factor = jnp.exp2(tops[b] - best)
            total += factor * sums[b]
            dot += factor * dots[b]
        st_send[n, 0:1, :] = best + jnp.log2(total)
        st_send[n, 1:2, :] = dot / total
        for delta in STAT_FROM:
            @pl.when(exists(delta))
            def _():
                st_copy(n, delta).start()

    def second(n):
        par = lax.rem(n, LAG + 1)
        for delta in STAT_FROM:
            @pl.when(exists(delta))
            def _():
                st_copy(n, -delta).wait_recv()
        logs = [st_send[n, 0:1, :]]
        dots = [st_send[n, 1:2, :]]
        for at, delta in enumerate(STAT_FROM):
            shared = (hop_of >= delta) if delta > 0 else (hop_of <= HOPS - 1 + delta)
            shared = jnp.logical_and(shared, exists(delta))
            logs.append(jnp.where(shared, st_recv[n, at, 0:1, :], -1e30))
            dots.append(jnp.where(shared, st_recv[n, at, 1:2, :], 0.0))
        best = logs[0]
        for x in logs[1:]:
            best = jnp.maximum(best, x)
        total = jnp.zeros_like(best)
        delta_row = jnp.zeros_like(best)
        for x, d in zip(logs, dots):
            factor = jnp.exp2(x - best)
            total += factor
            delta_row += factor * d
        delta_row = delta_row / total
        log_all = best + jnp.log2(total)
        for b in range(3):
            factor = jnp.exp2(top[par, b] - log_all)
            w = prob[par, b] * factor
            wb[b] = w.astype(BF16)
            ds[b] = (w * (dprob[par, b] - delta_row)).astype(BF16)
        w_all = wb[...].reshape(KEYS, QUERIES)
        s_all = ds[...].reshape(KEYS, QUERIES)
        q = qg[n, :, 0].reshape(QUERIES, DIM)
        g = qg[n, :, 1].reshape(QUERIES, DIM)
        dv = jnp.dot(w_all, g, preferred_element_type=F32)
        dk = jnp.dot(s_all, q, preferred_element_type=F32) * SCALE
        for to, b in ((0, 0), (1, 2)):
            rk_send[n, to, 0] = dk[b * ROWS:(b + 1) * ROWS].astype(BF16)
            rk_send[n, to, 1] = dv[b * ROWS:(b + 1) * ROWS].astype(BF16)
        rk_start(n)
        own_kv[n, 0] = dk[ROWS:2 * ROWS]
        own_kv[n, 1] = dv[ROWS:2 * ROWS]
        k_all = kv[n, :, 0].reshape(KEYS, DIM)
        v_all = kv[n, :, 1].reshape(KEYS, DIM)
        out = tn_dot(v_all, w_all).T
        dq = (tn_dot(k_all, s_all) * SCALE).T
        oq[n, :, 0] = out.astype(BF16).reshape(HOPS, ROWS, DIM)
        oq[n, :, 1] = dq.astype(BF16).reshape(HOPS, ROWS, DIM)
        rq_send(n, 3)

    def when_head(n, do, *rest):
        @pl.when(jnp.logical_and(n >= 0, n < HEADS))
        def _():
            do(n, *rest)

    for n in range(2):
        qg_pass(n)
    for n in range(3):
        qg_forward(n, 1)
    for n in range(2):
        qg_forward(n, 2)

    @pl.loop(0, HEADS + 7)
    def _(t):
        for n in (2 * t + 4, 2 * t + 5):
            when_head(n, kv_send)
            when_head(n, qg_send, 0)
        for n in (2 * t + 2, 2 * t + 3):
            when_head(n, qg_pass)
        when_head(2 * t + 1, kv_forward)
        when_head(t + 3, qg_forward, 1)
        when_head(t + 2, qg_forward, 2)
        when_head(t, first)
        when_head(t - LAG, second)
        for h, late in ((3, 3), (2, 5), (1, 7)):
            @pl.when((t - late) & 1 == 1)
            def _():
                when_head(t - late, rq_over, h)

        when_head(t - 4, rq_pass, 2)
        when_head(t - 6, rq_pass, 1)

        @pl.when((t & 1) == 1)
        def _():
            when_head(t - 4, rk_forward)

    @pl.loop(0, HEADS)
    def _(n):
        for to in range(2):
            rk_copy(n, to).wait_recv()

        @pl.when(o > 0)
        def _():
            rq_wait(n, 0)

        cols = pl.ds(pl.multiple_of(n * DIM, DIM), DIM)
        for part, out in ((0, dk_out), (1, dv_out)):
            total = own_kv[n, part]
            for to in range(2):
                total += rk_recv[n, to, part].astype(F32)
            out[:, cols] = total.astype(BF16)
        for part, out in ((0, o_out), (1, dq_out)):
            out[:, cols] = (oq[n, slot, part].astype(F32) + rq_recv[n, 0, part].astype(F32)).astype(BF16)

    @pl.loop(0, HEADS)
    def _(n):
        for to in range(2):
            @pl.when(jnp.logical_not(relayed_to(n, to)))
            def _():
                kv_copy(n, to).wait_send()
                rk_copy(n, to).wait_send()

            @pl.when(relayed_to(n, to))
            def _():
                relay_copy(n, to).wait_send()

        @pl.when(jnp.logical_and(relays, (n & 1) == 1))
        def _():
            kv_forward_copy(n).wait_send()
            rk_forward_copy(n).wait_send()

        for h in range(HOPS - 1):
            @pl.when(qg_sends(n, h))
            def _():
                qg_copy(n, h).wait_send()

            @pl.when(exists(h + 1))
            def _():
                rq_copy(n, h + 1).wait_send()
        @pl.when(qg_crosses(n, 2))
        def _():
            qg_cross_copy(n, 2).wait_send()

        @pl.when(qg_relayed(n))
        def _():
            qg_relay_copy(n).wait_send()

        @pl.when(qg_passes(n))
        def _():
            qg_pass_copy(n).wait_send()

        @pl.when(jnp.logical_and(rq_passes, (n & 1) == 1))
        def _():
            for h in range(1, HOPS):
                rq_over_copy(n, h).wait_send()

        for delta in STAT_FROM:
            @pl.when(exists(delta))
            def _():
                st_copy(n, delta).wait_send()


def store(*refs):
    for a, b in zip(refs[:4], refs[4:]):
        b[...] = a[...]


def on_device(queries, keys, values, d_out):
    block = jax.ShapeDtypeStruct((ROWS, HEADS * DIM), BF16)
    vmem = pl.BlockSpec(memory_space=pltpu.VMEM)
    dma = pltpu.SemaphoreType.DMA
    results = pl.pallas_call(
        kernel,
        out_shape=(block,) * 4,
        in_specs=[pl.BlockSpec(memory_space=pl.ANY)] * 4,
        out_specs=(vmem,) * 4,
        scratch_shapes=[
            pltpu.VMEM((HEADS, 3, 2, ROWS, DIM), BF16),
            pltpu.VMEM((HEADS, HOPS, 2, ROWS, DIM), BF16),
            pltpu.VMEM((LAG + 1, 3, ROWS, QUERIES), F32),
            pltpu.VMEM((LAG + 1, 3, ROWS, QUERIES), F32),
            pltpu.VMEM((3, ROWS, QUERIES), BF16),
            pltpu.VMEM((3, ROWS, QUERIES), BF16),
            pltpu.VMEM((LAG + 1, 3, 1, QUERIES), F32),
            pltpu.VMEM((HEADS, 2, QUERIES), F32),
            pltpu.VMEM((HEADS, 6, 2, QUERIES), F32),
            pltpu.VMEM((HEADS, 2, ROWS, DIM), F32),
            pltpu.VMEM((HEADS, 2, 2, ROWS, DIM), BF16),
            pltpu.VMEM((HEADS, 2, 2, ROWS, DIM), BF16),
            pltpu.VMEM((HEADS // 2, 2, ROWS, DIM), BF16),
            pltpu.VMEM((HEADS, HOPS, 2, ROWS, DIM), BF16),
            pltpu.VMEM((HEADS, HOPS - 1, 2, ROWS, DIM), BF16),
            pltpu.VMEM((HEADS, 2, ROWS, DIM), BF16),
            pltpu.VMEM((HEADS // 2, HOPS - 1, 2, ROWS, DIM), BF16),
            dma((HEADS, 4)),
            dma((HEADS, 2)), dma((HEADS, 2)), dma((HEADS // 2,)),
            dma((HEADS, 3)), dma((HEADS, 3)), dma((HEADS,)), dma((HEADS,)), dma((HEADS,)),
            dma((HEADS, 6)), dma((HEADS, 6)),
            dma((HEADS, 2)), dma((HEADS, 2)),
            dma((HEADS // 2,)), dma((HEADS // 2,)), dma((HEADS // 2,)),
            dma((HEADS, 3)), dma((HEADS, 3)),
            dma((HEADS // 2, 3)), dma((HEADS // 2, 3)),
        ],
        compiler_params=pltpu.CompilerParams(
            collective_id=0, has_side_effects=True, vmem_limit_bytes=56 << 20
        ),
        cost_estimate=pl.CostEstimate(
            flops=12 * HEADS * KEYS * QUERIES * DIM,
            bytes_accessed=8 * ROWS * HEADS * DIM * 2,
            transcendentals=HEADS * KEYS * QUERIES,
        ),
        name="window_attention",
    )(queries, keys, values, d_out)
    return pl.pallas_call(
        store,
        out_shape=(block,) * 4,
        in_specs=[vmem] * 4,
        out_specs=(vmem,) * 4,
        name="store_results",
    )(*results)


def solution(mesh):
    placed = P(("outer", "inner"), None)
    return jax.shard_map(
        on_device,
        mesh=mesh,
        in_specs=(placed,) * 4,
        out_specs=(placed,) * 4,
        check_vma=False,
    )
```

```python
import jax
import jax.numpy as jnp
from jax import lax
from jax.experimental import pallas as pl
from jax.experimental.pallas import tpu as pltpu
from jax.sharding import PartitionSpec as P

HEADS = 8
DIM = 128
HOPS = 4
ROWS = 192
KEYS = 3 * ROWS
QUERIES = HOPS * ROWS
TILE = 256
SCALE = DIM ** (-0.5)
LOG2E = 1.4426950408889634
RUN = 16
LAG = 1
TURN_RING = (1, 3, 5, 6)
TURN_RUN = (1, 3, 5, 6)
STAT_FROM = (-3, -2, -1, 1, 2, 3)
MESH = pl.DeviceIdType.MESH
F32 = jnp.float32
BF16 = jnp.bfloat16


def among(n, heads):
    found = n == heads[0]
    for head in heads[1:]:
        found = jnp.logical_or(found, n == head)
    return found


def nt_dot(a, b):
    return lax.dot_general(a, b, (((1,), (1,)), ((), ())), preferred_element_type=F32)


def tn_dot(a, b):
    return lax.dot_general(a, b, (((0,), (0,)), ((), ())), preferred_element_type=F32)


def kernel(
    q_in, k_in, v_in, g_in,
    o_out, dq_out, dk_out, dv_out,
    kv, qg, prob, dprob, wb, ds, top, st_send, st_recv,
    own_kv, rk_send, rk_recv, relayed, oq, rq_recv, q_held, r_held,
    load_sem, kv_ss, kv_rs, kv_fs, qg_ss, qg_rs, qg_xs, ql_rs, ql_fs, st_ss, st_rs,
    rk_ss, rk_rs, re_ss, re_rs, rk_fs, rq_ss, rq_rs, rl_rs, rl_fs,
):
    o = lax.axis_index("outer")
    i = lax.axis_index("inner")
    n_outer = lax.axis_size("outer")
    n_inner = lax.axis_size("inner")
    left = lax.rem(i + n_inner - 1, n_inner)
    right = lax.rem(i + 1, n_inner)
    slot = lax.rem(o, HOPS)
    place = lax.rem(o, RUN)
    early, last = place <= HOPS - 2, place == RUN - 1
    run_before, run_after = o >= RUN, o < n_outer - RUN
    ends = jnp.logical_or(early, last)
    x = lax.rem(i, 4)
    first_x, last_x = x == 0, x == 3
    relays = jnp.logical_or(x == 1, x == 2)
    up = (x == 2).astype(jnp.int32)
    far = lax.rem(jnp.where(x >= 2, i + 2, i + n_inner - 2), n_inner)

    def exists(delta):
        return o + delta >= 0 if delta < 0 else o + delta < n_outer

    def load(n):
        cols = pl.ds(pl.multiple_of(n * DIM, DIM), DIM)
        return (
            pltpu.make_async_copy(k_in.at[:, cols], kv.at[n, 1, 0], load_sem.at[n, 0]),
            pltpu.make_async_copy(v_in.at[:, cols], kv.at[n, 1, 1], load_sem.at[n, 1]),
            pltpu.make_async_copy(q_in.at[:, cols], qg.at[n, slot, 0], load_sem.at[n, 2]),
            pltpu.make_async_copy(g_in.at[:, cols], qg.at[n, slot, 1], load_sem.at[n, 3]),
        )

    @pl.loop(0, HEADS)
    def _(n):
        for copy in load(n):
            copy.start()

    barrier = pltpu.get_barrier_semaphore()
    for other in (left, right, far):
        pl.semaphore_signal(barrier, inc=1, device_id=(o, other), device_id_type=MESH)
    for delta in STAT_FROM:
        @pl.when(exists(delta))
        def _():
            pl.semaphore_signal(barrier, inc=1, device_id=(o + delta, i), device_id_type=MESH)

    @pl.when(jnp.logical_and(ends, run_before))
    def _():
        pl.semaphore_signal(barrier, inc=1, device_id=(o - RUN, i), device_id_type=MESH)

    @pl.when(jnp.logical_and(ends, run_after))
    def _():
        pl.semaphore_signal(barrier, inc=1, device_id=(o + RUN, i), device_id_type=MESH)

    @pl.when(early)
    def _():
        pl.semaphore_signal(barrier, inc=1, device_id=(o + RUN - 1 - place, i), device_id_type=MESH)

    @pl.when(last)
    def _():
        for p in range(HOPS - 1):
            pl.semaphore_signal(barrier, inc=1, device_id=(o - RUN + 1 + p, i), device_id_type=MESH)

    for h in range(1, HOPS):
        @pl.when(jnp.logical_not(exists(h)))
        def _():
            qg[:, lax.rem(o + h, HOPS)] = jnp.zeros((HEADS, 2, ROWS, DIM), BF16)
    for at, delta in enumerate(STAT_FROM):
        @pl.when(jnp.logical_not(exists(delta)))
        def _():
            st_recv[:, at] = jnp.zeros((HEADS, 2, QUERIES), F32)

    @pl.when(o == 0)
    def _():
        rq_recv[:, 0] = jnp.zeros((HEADS, 2, ROWS, DIM), BF16)

    behind = jnp.minimum(o, HOPS - 1)
    ahead = jnp.minimum(n_outer - 1 - o, HOPS - 1)
    across = run_before.astype(jnp.int32) + run_after.astype(jnp.int32)
    more = jnp.where(early, 1 + across, jnp.where(last, HOPS - 1 + across, 0))
    pl.semaphore_wait(barrier, 3 + behind + ahead + more)

    def kv_copy(n, to):
        return pltpu.make_async_remote_copy(
            kv.at[n, 1], kv.at[n, 2 - 2 * to], kv_ss.at[n, to], kv_rs.at[n, to],
            device_id=(o, (left, right)[to]), device_id_type=MESH,
        )

    def relayed_to(n, to):
        return jnp.logical_and((first_x, last_x)[to], among(n, TURN_RING))

    def kv_send(n):
        for to in range(2):
            @pl.when(jnp.logical_not(relayed_to(n, to)))
            def _():
                kv_copy(n, to).start()

    def kv_forward_copy(n):
        return pltpu.make_async_remote_copy(
            kv.at[n, 2 * up], kv.at[n, 2 - 2 * up], kv_fs.at[n >> 1], kv_rs.at[n, up],
            device_id=(o, far), device_id_type=MESH,
        )

    def kv_forward(n):
        @pl.when(x == 1)
        def _():
            kv_copy(n, 1).wait_recv()

        @pl.when(x == 2)
        def _():
            kv_copy(n, 0).wait_recv()

        @pl.when(relays)
        def _():
            kv_forward_copy(n).start()

    def kv_wait(n):
        odd = among(n, TURN_RING)
        for to in range(2):
            @pl.when(jnp.logical_not(jnp.logical_and(x == 2 - to, odd)))
            def _():
                kv_copy(n, to).wait_recv()

    def qg_copy(n, h):
        at = lax.rem(o + h, HOPS)
        return pltpu.make_async_remote_copy(
            qg.at[n, at], qg.at[n, at], qg_ss.at[n, h], qg_rs.at[n, h],
            device_id=(o - 1, i), device_id_type=MESH,
        )

    def qg_turns(n):
        return jnp.logical_or(place == 2, jnp.logical_and(place < 2, among(n, TURN_RUN)))

    def qg_relayed(n):
        return jnp.logical_and(run_before, qg_turns(n))

    def qg_sends(n, h):
        here = jnp.logical_and(o > 0, exists(h))
        if h == 0:
            return jnp.logical_and(here, jnp.logical_not(jnp.logical_and(place == 0, qg_relayed(n))))
        return jnp.logical_and(here, place > 0)

    def qg_cross_copy(n, h):
        return pltpu.make_async_remote_copy(
            qg.at[n, slot], qg.at[n, slot], qg_xs.at[n], qg_rs.at[n, h - 1],
            device_id=(o - h, i), device_id_type=MESH,
        )

    def qg_crosses(n, h):
        here = jnp.logical_and(run_before, place == h - 1)
        return jnp.logical_and(here, jnp.logical_not(qg_turns(n)))

    def qg_relay_copy(n):
        return pltpu.make_async_remote_copy(
            qg.at[n, slot], q_held.at[n], qg_xs.at[n], ql_rs.at[n],
            device_id=(o - RUN, i), device_id_type=MESH,
        )

    def qg_pass_copy(n):
        return pltpu.make_async_remote_copy(
            q_held.at[n], qg.at[n, slot], ql_fs.at[n], qg_rs.at[n, place],
            device_id=(o + RUN - 1 - place, i), device_id_type=MESH,
        )

    def qg_passes(n):
        return jnp.logical_and(run_after, qg_turns(n))

    def qg_pass(n):
        @pl.when(qg_passes(n))
        def _():
            qg_relay_copy(n).wait_recv()
            qg_pass_copy(n).start()

    def qg_send(n, h):
        @pl.when(qg_sends(n, h))
        def _():
            qg_copy(n, h).start()

        if h == 0:
            @pl.when(qg_crosses(n, 2))
            def _():
                qg_cross_copy(n, 2).start()

            @pl.when(qg_relayed(n))
            def _():
                qg_relay_copy(n).start()

    def qg_wait(n, h):
        at = lax.rem(o + h, HOPS)

        @pl.when(exists(h))
        def _():
            pltpu.make_async_remote_copy(
                qg.at[n, at], qg.at[n, at], qg_ss.at[n, h - 1], qg_rs.at[n, h - 1],
                device_id=(o - 1, i), device_id_type=MESH,
            ).wait_recv()

    def qg_forward(n, h):
        qg_wait(n, h)
        qg_send(n, h)

    def st_copy(n, delta):
        at = STAT_FROM.index(-delta)
        return pltpu.make_async_remote_copy(
            st_send.at[n], st_recv.at[n, at], st_ss.at[n, at], st_rs.at[n, at],
            device_id=(o + delta, i), device_id_type=MESH,
        )

    def rk_copy(n, to):
        return pltpu.make_async_remote_copy(
            rk_send.at[n, to], rk_recv.at[n, to], rk_ss.at[n, to], rk_rs.at[n, to],
            device_id=(o, (left, right)[to]), device_id_type=MESH,
        )

    def relay_copy(n, to):
        return pltpu.make_async_remote_copy(
            rk_send.at[n, to], relayed.at[n >> 1], re_ss.at[n >> 1], re_rs.at[n >> 1],
            device_id=(o, (right, left)[to]), device_id_type=MESH,
        )

    def rk_start(n):
        for to in range(2):
            @pl.when(jnp.logical_not(relayed_to(n, to)))
            def _():
                rk_copy(n, to).start()

            @pl.when(relayed_to(n, to))
            def _():
                relay_copy(n, to).start()

    def rk_forward_copy(n):
        return pltpu.make_async_remote_copy(
            relayed.at[n >> 1], rk_recv.at[n, up], rk_fs.at[n >> 1], rk_rs.at[n, up],
            device_id=(o, far), device_id_type=MESH,
        )

    def rk_forward(n):
        @pl.when(relays)
        def _():
            relay_copy(n, 0).wait_recv()
            rk_forward_copy(n).start()

    def rq_copy(n, h):
        return pltpu.make_async_remote_copy(
            oq.at[n, lax.rem(o + h, HOPS)], rq_recv.at[n, h - 1],
            rq_ss.at[n, h - 1], rq_rs.at[n, h - 1],
            device_id=(o + 1, i), device_id_type=MESH,
        )

    def rq_relay_copy(n, h):
        return pltpu.make_async_remote_copy(
            oq.at[n, lax.rem(o + h, HOPS)], r_held.at[n >> 1, h - 1],
            rq_ss.at[n, h - 1], rl_rs.at[n >> 1, h - 1],
            device_id=(o + RUN, i), device_id_type=MESH,
        )

    def rq_over_copy(n, h):
        return pltpu.make_async_remote_copy(
            r_held.at[n >> 1, h - 1], rq_recv.at[n, h - 1],
            rl_fs.at[n >> 1, h - 1], rq_rs.at[n, h - 1],
            device_id=(o - RUN + 1, i), device_id_type=MESH,
        )

    rq_passes = jnp.logical_and(last, run_before)

    def rq_over(n, h):
        @pl.when(rq_passes)
        def _():
            rq_relay_copy(n, h).wait_recv()
            rq_over_copy(n, h).start()

    def rq_relayed(n):
        return jnp.logical_and(last, among(n, TURN_RUN))

    def rq_send(n, h):
        @pl.when(jnp.logical_and(exists(h), rq_relayed(n)))
        def _():
            rq_relay_copy(n, h).start()

        @pl.when(jnp.logical_and(exists(h), jnp.logical_not(rq_relayed(n))))
        def _():
            rq_copy(n, h).start()

    def rq_wait(n, h):
        pltpu.make_async_remote_copy(
            oq.at[n, 0], rq_recv.at[n, h], rq_ss.at[n, h], rq_rs.at[n, h],
            device_id=(o + 1, i), device_id_type=MESH,
        ).wait_recv()

    def rq_pass(n, h):
        at = lax.rem(o + h, HOPS)

        @pl.when(jnp.logical_and(o > 0, exists(h)))
        def _():
            rq_wait(n, h)
            oq[n, at] = (oq[n, at].astype(F32) + rq_recv[n, h].astype(F32)).astype(BF16)

        rq_send(n, h)

    for n in range(HEADS):
        for copy in load(n):
            copy.wait()
        if n < 4:
            kv_send(n)
            qg_send(n, 0)

    lane = lax.broadcasted_iota(jnp.int32, (1, QUERIES), 1)
    at_slot = sum((lane >= ROWS * s).astype(jnp.int32) for s in range(1, HOPS))
    hop_of = (at_slot - slot + HOPS) & (HOPS - 1)

    def first(n):
        par = lax.rem(n, LAG + 1)
        kv_wait(n)
        qg_wait(n, 3)
        q = qg[n, :, 0].reshape(QUERIES, DIM)
        g = qg[n, :, 1].reshape(QUERIES, DIM)
        tops, sums, dots = [], [], []
        for b in range(3):
            k = kv[n, b, 0]
            v = kv[n, b, 1]
            t_row, s_row, d_row = [], [], []
            for t in range(QUERIES // TILE):
                cols = slice(t * TILE, (t + 1) * TILE)
                s = nt_dot(k, q[cols])
                high = jnp.max(s, axis=0, keepdims=True)
                p = jnp.exp2((s - high) * (SCALE * LOG2E))
                dp = nt_dot(v, g[cols])
                prob[par, b, :, cols] = p
                dprob[par, b, :, cols] = dp
                t_row.append(high * (SCALE * LOG2E))
                s_row.append(jnp.sum(p, axis=0, keepdims=True))
                d_row.append(jnp.sum(p * dp, axis=0, keepdims=True))
            tops.append(jnp.concatenate(t_row, axis=1))
            sums.append(jnp.concatenate(s_row, axis=1))
            dots.append(jnp.concatenate(d_row, axis=1))
            top[par, b] = tops[-1]
        best = jnp.maximum(jnp.maximum(tops[0], tops[1]), tops[2])
        total = jnp.zeros_like(best)
        dot = jnp.zeros_like(best)
        for b in range(3):
            factor = jnp.exp2(tops[b] - best)
            total += factor * sums[b]
            dot += factor * dots[b]
        st_send[n, 0:1, :] = best + jnp.log2(total)
        st_send[n, 1:2, :] = dot / total
        for delta in STAT_FROM:
            @pl.when(exists(delta))
            def _():
                st_copy(n, delta).start()

    def second(n):
        par = lax.rem(n, LAG + 1)
        for delta in STAT_FROM:
            @pl.when(exists(delta))
            def _():
                st_copy(n, -delta).wait_recv()
        logs = [st_send[n, 0:1, :]]
        dots = [st_send[n, 1:2, :]]
        for at, delta in enumerate(STAT_FROM):
            shared = (hop_of >= delta) if delta > 0 else (hop_of <= HOPS - 1 + delta)
            shared = jnp.logical_and(shared, exists(delta))
            logs.append(jnp.where(shared, st_recv[n, at, 0:1, :], -1e30))
            dots.append(jnp.where(shared, st_recv[n, at, 1:2, :], 0.0))
        best = logs[0]
        for x in logs[1:]:
            best = jnp.maximum(best, x)
        total = jnp.zeros_like(best)
        delta_row = jnp.zeros_like(best)
        for x, d in zip(logs, dots):
            factor = jnp.exp2(x - best)
            total += factor
            delta_row += factor * d
        delta_row = delta_row / total
        log_all = best + jnp.log2(total)
        for b in range(3):
            factor = jnp.exp2(top[par, b] - log_all)
            w = prob[par, b] * factor
            wb[b] = w.astype(BF16)
            ds[b] = (w * (dprob[par, b] - delta_row)).astype(BF16)
        w_all = wb[...].reshape(KEYS, QUERIES)
        s_all = ds[...].reshape(KEYS, QUERIES)
        q = qg[n, :, 0].reshape(QUERIES, DIM)
        g = qg[n, :, 1].reshape(QUERIES, DIM)
        dv = jnp.dot(w_all, g, preferred_element_type=F32)
        dk = jnp.dot(s_all, q, preferred_element_type=F32) * SCALE
        for to, b in ((0, 0), (1, 2)):
            rk_send[n, to, 0] = dk[b * ROWS:(b + 1) * ROWS].astype(BF16)
            rk_send[n, to, 1] = dv[b * ROWS:(b + 1) * ROWS].astype(BF16)
        rk_start(n)
        own_kv[n, 0] = dk[ROWS:2 * ROWS]
        own_kv[n, 1] = dv[ROWS:2 * ROWS]
        k_all = kv[n, :, 0].reshape(KEYS, DIM)
        v_all = kv[n, :, 1].reshape(KEYS, DIM)
        out = tn_dot(v_all, w_all).T
        dq = (tn_dot(k_all, s_all) * SCALE).T
        oq[n, :, 0] = out.astype(BF16).reshape(HOPS, ROWS, DIM)
        oq[n, :, 1] = dq.astype(BF16).reshape(HOPS, ROWS, DIM)
        rq_send(n, 3)

    def when_head(n, do, *rest):
        @pl.when(jnp.logical_and(n >= 0, n < HEADS))
        def _():
            do(n, *rest)

    for n in range(2):
        qg_pass(n)
    for n in range(3):
        qg_forward(n, 1)
    for n in range(2):
        qg_forward(n, 2)

    @pl.loop(0, HEADS + 6)
    def _(t):
        for n in (2 * t + 4, 2 * t + 5):
            when_head(n, kv_send)
            when_head(n, qg_send, 0)
        for n in (2 * t + 2, 2 * t + 3):
            when_head(n, qg_pass)
        for n in (2 * t, 2 * t + 1):
            @pl.when(among(n, TURN_RING))
            def _():
                kv_forward(n)

        when_head(t + 3, qg_forward, 1)
        when_head(t + 2, qg_forward, 2)
        @pl.when(among(t - 3, TURN_RING))
        def _():
            rk_forward(t - 3)

        when_head(t, first)
        when_head(t - LAG, second)
        for h, late in ((3, 2), (2, 4), (1, 6)):
            @pl.when(among(t - late, TURN_RUN))
            def _():
                rq_over(t - late, h)

        when_head(t - 3, rq_pass, 2)
        when_head(t - 5, rq_pass, 1)

    @pl.loop(0, HEADS)
    def _(n):
        for to in range(2):
            rk_copy(n, to).wait_recv()

        @pl.when(o > 0)
        def _():
            rq_wait(n, 0)

        cols = pl.ds(pl.multiple_of(n * DIM, DIM), DIM)
        for part, out in ((0, dk_out), (1, dv_out)):
            total = own_kv[n, part]
            for to in range(2):
                total += rk_recv[n, to, part].astype(F32)
            out[:, cols] = total.astype(BF16)
        for part, out in ((0, o_out), (1, dq_out)):
            out[:, cols] = (oq[n, slot, part].astype(F32) + rq_recv[n, 0, part].astype(F32)).astype(BF16)

    @pl.loop(0, HEADS)
    def _(n):
        for to in range(2):
            @pl.when(jnp.logical_not(relayed_to(n, to)))
            def _():
                kv_copy(n, to).wait_send()
                rk_copy(n, to).wait_send()

            @pl.when(relayed_to(n, to))
            def _():
                relay_copy(n, to).wait_send()

        @pl.when(jnp.logical_and(relays, among(n, TURN_RING)))
        def _():
            kv_forward_copy(n).wait_send()
            rk_forward_copy(n).wait_send()

        for h in range(HOPS - 1):
            @pl.when(qg_sends(n, h))
            def _():
                qg_copy(n, h).wait_send()

            @pl.when(exists(h + 1))
            def _():
                rq_copy(n, h + 1).wait_send()
        @pl.when(qg_crosses(n, 2))
        def _():
            qg_cross_copy(n, 2).wait_send()

        @pl.when(qg_relayed(n))
        def _():
            qg_relay_copy(n).wait_send()

        @pl.when(qg_passes(n))
        def _():
            qg_pass_copy(n).wait_send()

        @pl.when(jnp.logical_and(rq_passes, among(n, TURN_RUN)))
        def _():
            for h in range(1, HOPS):
                rq_over_copy(n, h).wait_send()

        for delta in STAT_FROM:
            @pl.when(exists(delta))
            def _():
                st_copy(n, delta).wait_send()


def store(*refs):
    for a, b in zip(refs[:4], refs[4:]):
        b[...] = a[...]


def on_device(queries, keys, values, d_out):
    block = jax.ShapeDtypeStruct((ROWS, HEADS * DIM), BF16)
    vmem = pl.BlockSpec(memory_space=pltpu.VMEM)
    dma = pltpu.SemaphoreType.DMA
    results = pl.pallas_call(
        kernel,
        out_shape=(block,) * 4,
        in_specs=[pl.BlockSpec(memory_space=pl.ANY)] * 4,
        out_specs=(vmem,) * 4,
        scratch_shapes=[
            pltpu.VMEM((HEADS, 3, 2, ROWS, DIM), BF16),
            pltpu.VMEM((HEADS, HOPS, 2, ROWS, DIM), BF16),
            pltpu.VMEM((LAG + 1, 3, ROWS, QUERIES), F32),
            pltpu.VMEM((LAG + 1, 3, ROWS, QUERIES), F32),
            pltpu.VMEM((3, ROWS, QUERIES), BF16),
            pltpu.VMEM((3, ROWS, QUERIES), BF16),
            pltpu.VMEM((LAG + 1, 3, 1, QUERIES), F32),
            pltpu.VMEM((HEADS, 2, QUERIES), F32),
            pltpu.VMEM((HEADS, 6, 2, QUERIES), F32),
            pltpu.VMEM((HEADS, 2, ROWS, DIM), F32),
            pltpu.VMEM((HEADS, 2, 2, ROWS, DIM), BF16),
            pltpu.VMEM((HEADS, 2, 2, ROWS, DIM), BF16),
            pltpu.VMEM((HEADS // 2, 2, ROWS, DIM), BF16),
            pltpu.VMEM((HEADS, HOPS, 2, ROWS, DIM), BF16),
            pltpu.VMEM((HEADS, HOPS - 1, 2, ROWS, DIM), BF16),
            pltpu.VMEM((HEADS, 2, ROWS, DIM), BF16),
            pltpu.VMEM((HEADS // 2, HOPS - 1, 2, ROWS, DIM), BF16),
            dma((HEADS, 4)),
            dma((HEADS, 2)), dma((HEADS, 2)), dma((HEADS // 2,)),
            dma((HEADS, 3)), dma((HEADS, 3)), dma((HEADS,)), dma((HEADS,)), dma((HEADS,)),
            dma((HEADS, 6)), dma((HEADS, 6)),
            dma((HEADS, 2)), dma((HEADS, 2)),
            dma((HEADS // 2,)), dma((HEADS // 2,)), dma((HEADS // 2,)),
            dma((HEADS, 3)), dma((HEADS, 3)),
            dma((HEADS // 2, 3)), dma((HEADS // 2, 3)),
        ],
        compiler_params=pltpu.CompilerParams(
            collective_id=0, has_side_effects=True, vmem_limit_bytes=56 << 20
        ),
        cost_estimate=pl.CostEstimate(
            flops=12 * HEADS * KEYS * QUERIES * DIM,
            bytes_accessed=8 * ROWS * HEADS * DIM * 2,
            transcendentals=HEADS * KEYS * QUERIES,
        ),
        name="window_attention",
    )(queries, keys, values, d_out)
    return pl.pallas_call(
        store,
        out_shape=(block,) * 4,
        in_specs=[vmem] * 4,
        out_specs=(vmem,) * 4,
        name="store_results",
    )(*results)


def solution(mesh):
    placed = P(("outer", "inner"), None)
    return jax.shard_map(
        on_device,
        mesh=mesh,
        in_specs=(placed,) * 4,
        out_specs=(placed,) * 4,
        check_vma=False,
    )
```

```python
import jax
import jax.numpy as jnp
from jax import lax
from jax.experimental import pallas as pl
from jax.experimental.pallas import tpu as pltpu
from jax.sharding import PartitionSpec as P

HEADS = 8
DIM = 128
HOPS = 4
ROWS = 192
KEYS = 3 * ROWS
QUERIES = HOPS * ROWS
TILE = 256
SCALE = DIM ** (-0.5)
LOG2E = 1.4426950408889634
RUN = 16
LAG = 1
TURN_RING = (1, 3, 5, 6)
TURN_RUN = (1, 3, 5, 6)
STAT_FROM = (-3, -2, -1, 1, 2, 3)
MESH = pl.DeviceIdType.MESH
F32 = jnp.float32
BF16 = jnp.bfloat16


def among(n, heads):
    found = n == heads[0]
    for head in heads[1:]:
        found = jnp.logical_or(found, n == head)
    return found


def nt_dot(a, b):
    return lax.dot_general(a, b, (((1,), (1,)), ((), ())), preferred_element_type=F32)


def tn_dot(a, b):
    return lax.dot_general(a, b, (((0,), (0,)), ((), ())), preferred_element_type=F32)


def kernel(
    q_in, k_in, v_in, g_in,
    o_out, dq_out, dk_out, dv_out,
    kv, qg, prob, dprob, wb, ds, top, st_send, st_recv,
    own_kv, rk_send, rk_recv, relayed, oq, rq_recv, q_held, r_held,
    load_sem, kv_ss, kv_rs, kv_fs, qg_ss, qg_rs, qg_xs, ql_rs, ql_fs, st_ss, st_rs,
    rk_ss, rk_rs, re_ss, re_rs, rk_fs, rq_ss, rq_rs, rl_rs, rl_fs,
):
    o = lax.axis_index("outer")
    i = lax.axis_index("inner")
    n_outer = lax.axis_size("outer")
    n_inner = lax.axis_size("inner")
    left = lax.rem(i + n_inner - 1, n_inner)
    right = lax.rem(i + 1, n_inner)
    slot = lax.rem(o, HOPS)
    place = lax.rem(o, RUN)
    early, last = place <= HOPS - 2, place == RUN - 1
    run_before, run_after = o >= RUN, o < n_outer - RUN
    ends = jnp.logical_or(early, last)
    x = lax.rem(i, 4)
    first_x, last_x = x == 0, x == 3
    relays = jnp.logical_or(x == 1, x == 2)
    up = (x == 2).astype(jnp.int32)
    far = lax.rem(jnp.where(x >= 2, i + 2, i + n_inner - 2), n_inner)

    def exists(delta):
        return o + delta >= 0 if delta < 0 else o + delta < n_outer

    def load(n):
        cols = pl.ds(pl.multiple_of(n * DIM, DIM), DIM)
        return (
            pltpu.make_async_copy(k_in.at[:, cols], kv.at[n, 1, 0], load_sem.at[n, 0]),
            pltpu.make_async_copy(v_in.at[:, cols], kv.at[n, 1, 1], load_sem.at[n, 1]),
            pltpu.make_async_copy(q_in.at[:, cols], qg.at[n, slot, 0], load_sem.at[n, 2]),
            pltpu.make_async_copy(g_in.at[:, cols], qg.at[n, slot, 1], load_sem.at[n, 3]),
        )

    @pl.loop(0, HEADS)
    def _(n):
        for copy in load(n):
            copy.start()

    barrier = pltpu.get_barrier_semaphore()
    for other in (left, right, far):
        pl.semaphore_signal(barrier, inc=1, device_id=(o, other), device_id_type=MESH)
    for delta in STAT_FROM:
        @pl.when(exists(delta))
        def _():
            pl.semaphore_signal(barrier, inc=1, device_id=(o + delta, i), device_id_type=MESH)

    @pl.when(jnp.logical_and(ends, run_before))
    def _():
        pl.semaphore_signal(barrier, inc=1, device_id=(o - RUN, i), device_id_type=MESH)

    @pl.when(jnp.logical_and(ends, run_after))
    def _():
        pl.semaphore_signal(barrier, inc=1, device_id=(o + RUN, i), device_id_type=MESH)

    @pl.when(early)
    def _():
        pl.semaphore_signal(barrier, inc=1, device_id=(o + RUN - 1 - place, i), device_id_type=MESH)

    @pl.when(last)
    def _():
        for p in range(HOPS - 1):
            pl.semaphore_signal(barrier, inc=1, device_id=(o - RUN + 1 + p, i), device_id_type=MESH)

    for h in range(1, HOPS):
        @pl.when(jnp.logical_not(exists(h)))
        def _():
            qg[:, lax.rem(o + h, HOPS)] = jnp.zeros((HEADS, 2, ROWS, DIM), BF16)
    for at, delta in enumerate(STAT_FROM):
        @pl.when(jnp.logical_not(exists(delta)))
        def _():
            st_recv[:, at] = jnp.zeros((HEADS, 2, QUERIES), F32)

    @pl.when(o == 0)
    def _():
        rq_recv[:, 0] = jnp.zeros((HEADS, 2, ROWS, DIM), BF16)

    behind = jnp.minimum(o, HOPS - 1)
    ahead = jnp.minimum(n_outer - 1 - o, HOPS - 1)
    across = run_before.astype(jnp.int32) + run_after.astype(jnp.int32)
    more = jnp.where(early, 1 + across, jnp.where(last, HOPS - 1 + across, 0))
    pl.semaphore_wait(barrier, 3 + behind + ahead + more)

    def kv_copy(n, to):
        return pltpu.make_async_remote_copy(
            kv.at[n, 1], kv.at[n, 2 - 2 * to], kv_ss.at[n, to], kv_rs.at[n, to],
            device_id=(o, (left, right)[to]), device_id_type=MESH,
        )

    def relayed_to(n, to):
        return jnp.logical_and((first_x, last_x)[to], among(n, TURN_RING))

    def kv_send(n):
        for to in range(2):
            @pl.when(jnp.logical_not(relayed_to(n, to)))
            def _():
                kv_copy(n, to).start()

    def kv_forward_copy(n):
        return pltpu.make_async_remote_copy(
            kv.at[n, 2 * up], kv.at[n, 2 - 2 * up], kv_fs.at[n >> 1], kv_rs.at[n, up],
            device_id=(o, far), device_id_type=MESH,
        )

    def kv_forward(n):
        @pl.when(x == 1)
        def _():
            kv_copy(n, 1).wait_recv()

        @pl.when(x == 2)
        def _():
            kv_copy(n, 0).wait_recv()

        @pl.when(relays)
        def _():
            kv_forward_copy(n).start()

    def kv_wait(n):
        odd = among(n, TURN_RING)
        for to in range(2):
            @pl.when(jnp.logical_not(jnp.logical_and(x == 2 - to, odd)))
            def _():
                kv_copy(n, to).wait_recv()

    def qg_copy(n, h):
        at = lax.rem(o + h, HOPS)
        return pltpu.make_async_remote_copy(
            qg.at[n, at], qg.at[n, at], qg_ss.at[n, h], qg_rs.at[n, h],
            device_id=(o - 1, i), device_id_type=MESH,
        )

    def qg_turns(n):
        return jnp.logical_or(place == 2, jnp.logical_and(place < 2, among(n, TURN_RUN)))

    def qg_relayed(n):
        return jnp.logical_and(run_before, qg_turns(n))

    def qg_sends(n, h):
        here = jnp.logical_and(o > 0, exists(h))
        if h == 0:
            return jnp.logical_and(here, jnp.logical_not(jnp.logical_and(place == 0, qg_relayed(n))))
        return jnp.logical_and(here, place > 0)

    def qg_cross_copy(n, h):
        return pltpu.make_async_remote_copy(
            qg.at[n, slot], qg.at[n, slot], qg_xs.at[n], qg_rs.at[n, h - 1],
            device_id=(o - h, i), device_id_type=MESH,
        )

    def qg_crosses(n, h):
        here = jnp.logical_and(run_before, place == h - 1)
        return jnp.logical_and(here, jnp.logical_not(qg_turns(n)))

    def qg_relay_copy(n):
        return pltpu.make_async_remote_copy(
            qg.at[n, slot], q_held.at[n], qg_xs.at[n], ql_rs.at[n],
            device_id=(o - RUN, i), device_id_type=MESH,
        )

    def qg_pass_copy(n):
        return pltpu.make_async_remote_copy(
            q_held.at[n], qg.at[n, slot], ql_fs.at[n], qg_rs.at[n, place],
            device_id=(o + RUN - 1 - place, i), device_id_type=MESH,
        )

    def qg_passes(n):
        return jnp.logical_and(run_after, qg_turns(n))

    def qg_pass(n):
        @pl.when(qg_passes(n))
        def _():
            qg_relay_copy(n).wait_recv()
            qg_pass_copy(n).start()

    def qg_send(n, h):
        @pl.when(qg_sends(n, h))
        def _():
            qg_copy(n, h).start()

        if h == 0:
            @pl.when(qg_crosses(n, 2))
            def _():
                qg_cross_copy(n, 2).start()

            @pl.when(qg_relayed(n))
            def _():
                qg_relay_copy(n).start()

    def qg_wait(n, h):
        at = lax.rem(o + h, HOPS)

        @pl.when(exists(h))
        def _():
            pltpu.make_async_remote_copy(
                qg.at[n, at], qg.at[n, at], qg_ss.at[n, h - 1], qg_rs.at[n, h - 1],
                device_id=(o - 1, i), device_id_type=MESH,
            ).wait_recv()

    def qg_forward(n, h):
        qg_wait(n, h)
        qg_send(n, h)

    def st_copy(n, delta):
        at = STAT_FROM.index(-delta)
        return pltpu.make_async_remote_copy(
            st_send.at[n], st_recv.at[n, at], st_ss.at[n, at], st_rs.at[n, at],
            device_id=(o + delta, i), device_id_type=MESH,
        )

    def rk_copy(n, to):
        return pltpu.make_async_remote_copy(
            rk_send.at[n, to], rk_recv.at[n, to], rk_ss.at[n, to], rk_rs.at[n, to],
            device_id=(o, (left, right)[to]), device_id_type=MESH,
        )

    def relay_copy(n, to):
        return pltpu.make_async_remote_copy(
            rk_send.at[n, to], relayed.at[n >> 1], re_ss.at[n >> 1], re_rs.at[n >> 1],
            device_id=(o, (right, left)[to]), device_id_type=MESH,
        )

    def rk_start(n):
        for to in range(2):
            @pl.when(jnp.logical_not(relayed_to(n, to)))
            def _():
                rk_copy(n, to).start()

            @pl.when(relayed_to(n, to))
            def _():
                relay_copy(n, to).start()

    def rk_forward_copy(n):
        return pltpu.make_async_remote_copy(
            relayed.at[n >> 1], rk_recv.at[n, up], rk_fs.at[n >> 1], rk_rs.at[n, up],
            device_id=(o, far), device_id_type=MESH,
        )

    def rk_forward(n):
        @pl.when(relays)
        def _():
            relay_copy(n, 0).wait_recv()
            rk_forward_copy(n).start()

    def rq_copy(n, h):
        return pltpu.make_async_remote_copy(
            oq.at[n, lax.rem(o + h, HOPS)], rq_recv.at[n, h - 1],
            rq_ss.at[n, h - 1], rq_rs.at[n, h - 1],
            device_id=(o + 1, i), device_id_type=MESH,
        )

    def rq_relay_copy(n, h):
        return pltpu.make_async_remote_copy(
            oq.at[n, lax.rem(o + h, HOPS)], r_held.at[n >> 1, h - 1],
            rq_ss.at[n, h - 1], rl_rs.at[n >> 1, h - 1],
            device_id=(o + RUN, i), device_id_type=MESH,
        )

    def rq_over_copy(n, h):
        return pltpu.make_async_remote_copy(
            r_held.at[n >> 1, h - 1], rq_recv.at[n, h - 1],
            rl_fs.at[n >> 1, h - 1], rq_rs.at[n, h - 1],
            device_id=(o - RUN + 1, i), device_id_type=MESH,
        )

    rq_passes = jnp.logical_and(last, run_before)

    def rq_over(n, h):
        @pl.when(rq_passes)
        def _():
            rq_relay_copy(n, h).wait_recv()
            rq_over_copy(n, h).start()

    def rq_relayed(n):
        return jnp.logical_and(last, among(n, TURN_RUN))

    def rq_send(n, h):
        @pl.when(jnp.logical_and(exists(h), rq_relayed(n)))
        def _():
            rq_relay_copy(n, h).start()

        @pl.when(jnp.logical_and(exists(h), jnp.logical_not(rq_relayed(n))))
        def _():
            rq_copy(n, h).start()

    def rq_wait(n, h):
        pltpu.make_async_remote_copy(
            oq.at[n, 0], rq_recv.at[n, h], rq_ss.at[n, h], rq_rs.at[n, h],
            device_id=(o + 1, i), device_id_type=MESH,
        ).wait_recv()

    def rq_pass(n, h):
        at = lax.rem(o + h, HOPS)

        @pl.when(jnp.logical_and(o > 0, exists(h)))
        def _():
            rq_wait(n, h)
            oq[n, at] = (oq[n, at].astype(F32) + rq_recv[n, h].astype(F32)).astype(BF16)

        rq_send(n, h)

    for n in range(HEADS):
        for copy in load(n):
            copy.wait()
        if n < 4:
            kv_send(n)
            qg_send(n, 0)

    lane = lax.broadcasted_iota(jnp.int32, (1, QUERIES), 1)
    at_slot = sum((lane >= ROWS * s).astype(jnp.int32) for s in range(1, HOPS))
    hop_of = (at_slot - slot + HOPS) & (HOPS - 1)

    def first(n):
        par = lax.rem(n, LAG + 1)
        kv_wait(n)
        qg_wait(n, 3)
        q = qg[n, :, 0].reshape(QUERIES, DIM)
        g = qg[n, :, 1].reshape(QUERIES, DIM)
        tops, sums, dots = [], [], []
        for b in range(3):
            k = kv[n, b, 0]
            v = kv[n, b, 1]
            t_row, s_row, d_row = [], [], []
            for t in range(QUERIES // TILE):
                cols = slice(t * TILE, (t + 1) * TILE)
                s = nt_dot(k, q[cols])
                high = jnp.max(s, axis=0, keepdims=True)
                p = jnp.exp2((s - high) * (SCALE * LOG2E))
                dp = nt_dot(v, g[cols])
                prob[par, b, :, cols] = p
                dprob[par, b, :, cols] = dp
                t_row.append(high * (SCALE * LOG2E))
                s_row.append(jnp.sum(p, axis=0, keepdims=True))
                d_row.append(jnp.sum(p * dp, axis=0, keepdims=True))
            tops.append(jnp.concatenate(t_row, axis=1))
            sums.append(jnp.concatenate(s_row, axis=1))
            dots.append(jnp.concatenate(d_row, axis=1))
            top[par, b] = tops[-1]
        best = jnp.maximum(jnp.maximum(tops[0], tops[1]), tops[2])
        total = jnp.zeros_like(best)
        dot = jnp.zeros_like(best)
        for b in range(3):
            factor = jnp.exp2(tops[b] - best)
            total += factor * sums[b]
            dot += factor * dots[b]
        st_send[n, 0:1, :] = best + jnp.log2(total)
        st_send[n, 1:2, :] = dot / total
        for delta in STAT_FROM:
            @pl.when(exists(delta))
            def _():
                st_copy(n, delta).start()

    def second(n):
        par = lax.rem(n, LAG + 1)
        for delta in STAT_FROM:
            @pl.when(exists(delta))
            def _():
                st_copy(n, -delta).wait_recv()
        logs = [st_send[n, 0:1, :]]
        dots = [st_send[n, 1:2, :]]
        for at, delta in enumerate(STAT_FROM):
            shared = (hop_of >= delta) if delta > 0 else (hop_of <= HOPS - 1 + delta)
            shared = jnp.logical_and(shared, exists(delta))
            logs.append(jnp.where(shared, st_recv[n, at, 0:1, :], -1e30))
            dots.append(jnp.where(shared, st_recv[n, at, 1:2, :], 0.0))
        best = logs[0]
        for x in logs[1:]:
            best = jnp.maximum(best, x)
        total = jnp.zeros_like(best)
        delta_row = jnp.zeros_like(best)
        for x, d in zip(logs, dots):
            factor = jnp.exp2(x - best)
            total += factor
            delta_row += factor * d
        delta_row = delta_row / total
        log_all = best + jnp.log2(total)
        for b in range(3):
            factor = jnp.exp2(top[par, b] - log_all)
            w = prob[par, b] * factor
            wb[b] = w.astype(BF16)
            ds[b] = (w * (dprob[par, b] - delta_row)).astype(BF16)
        w_all = wb[...].reshape(KEYS, QUERIES)
        s_all = ds[...].reshape(KEYS, QUERIES)
        q = qg[n, :, 0].reshape(QUERIES, DIM)
        g = qg[n, :, 1].reshape(QUERIES, DIM)
        dv = jnp.dot(w_all, g, preferred_element_type=F32)
        dk = jnp.dot(s_all, q, preferred_element_type=F32) * SCALE
        for to, b in ((0, 0), (1, 2)):
            rk_send[n, to, 0] = dk[b * ROWS:(b + 1) * ROWS].astype(BF16)
            rk_send[n, to, 1] = dv[b * ROWS:(b + 1) * ROWS].astype(BF16)
        rk_start(n)
        own_kv[n, 0] = dk[ROWS:2 * ROWS]
        own_kv[n, 1] = dv[ROWS:2 * ROWS]
        k_all = kv[n, :, 0].reshape(KEYS, DIM)
        v_all = kv[n, :, 1].reshape(KEYS, DIM)
        out = tn_dot(v_all, w_all).T
        dq = (tn_dot(k_all, s_all) * SCALE).T
        oq[n, :, 0] = out.astype(BF16).reshape(HOPS, ROWS, DIM)
        oq[n, :, 1] = dq.astype(BF16).reshape(HOPS, ROWS, DIM)
        rq_send(n, 3)

    def left_out(n):
        for to in range(2):
            @pl.when(jnp.logical_not(relayed_to(n, to)))
            def _():
                kv_copy(n, to).wait_send()

        @pl.when(jnp.logical_and(relays, among(n, TURN_RING)))
        def _():
            kv_forward_copy(n).wait_send()

        for h in range(HOPS - 1):
            @pl.when(qg_sends(n, h))
            def _():
                qg_copy(n, h).wait_send()

        @pl.when(qg_crosses(n, 2))
        def _():
            qg_cross_copy(n, 2).wait_send()

        @pl.when(qg_relayed(n))
        def _():
            qg_relay_copy(n).wait_send()

        @pl.when(qg_passes(n))
        def _():
            qg_pass_copy(n).wait_send()

        for delta in STAT_FROM:
            @pl.when(exists(delta))
            def _():
                st_copy(n, delta).wait_send()

    def when_head(n, do, *rest):
        @pl.when(jnp.logical_and(n >= 0, n < HEADS))
        def _():
            do(n, *rest)

    for n in range(2):
        qg_pass(n)
    for n in range(3):
        qg_forward(n, 1)
    for n in range(2):
        qg_forward(n, 2)

    @pl.loop(0, HEADS + 6)
    def _(t):
        for n in (2 * t + 4, 2 * t + 5):
            when_head(n, kv_send)
            when_head(n, qg_send, 0)
        for n in (2 * t + 2, 2 * t + 3):
            when_head(n, qg_pass)
        for n in (2 * t, 2 * t + 1):
            @pl.when(among(n, TURN_RING))
            def _():
                kv_forward(n)

        when_head(t + 3, qg_forward, 1)
        when_head(t + 2, qg_forward, 2)
        @pl.when(among(t - 3, TURN_RING))
        def _():
            rk_forward(t - 3)

        when_head(t, first)
        when_head(t - LAG, second)
        for h, late in ((3, 2), (2, 4), (1, 6)):
            @pl.when(among(t - late, TURN_RUN))
            def _():
                rq_over(t - late, h)

        when_head(t - 3, rq_pass, 2)
        when_head(t - 5, rq_pass, 1)
        when_head(t - 5, left_out)

    @pl.loop(0, HEADS)
    def _(n):
        for to in range(2):
            rk_copy(n, to).wait_recv()

        @pl.when(o > 0)
        def _():
            rq_wait(n, 0)

        cols = pl.ds(pl.multiple_of(n * DIM, DIM), DIM)
        for part, out in ((0, dk_out), (1, dv_out)):
            total = own_kv[n, part]
            for to in range(2):
                total += rk_recv[n, to, part].astype(F32)
            out[:, cols] = total.astype(BF16)
        for part, out in ((0, o_out), (1, dq_out)):
            out[:, cols] = (oq[n, slot, part].astype(F32) + rq_recv[n, 0, part].astype(F32)).astype(BF16)

    @pl.loop(0, HEADS)
    def _(n):
        for to in range(2):
            @pl.when(jnp.logical_not(relayed_to(n, to)))
            def _():
                rk_copy(n, to).wait_send()

            @pl.when(relayed_to(n, to))
            def _():
                relay_copy(n, to).wait_send()

        @pl.when(jnp.logical_and(relays, among(n, TURN_RING)))
        def _():
            rk_forward_copy(n).wait_send()

        for h in range(1, HOPS):
            @pl.when(exists(h))
            def _():
                rq_copy(n, h).wait_send()

        @pl.when(jnp.logical_and(rq_passes, among(n, TURN_RUN)))
        def _():
            for h in range(1, HOPS):
                rq_over_copy(n, h).wait_send()


def store(*refs):
    for a, b in zip(refs[:4], refs[4:]):
        b[...] = a[...]


def on_device(queries, keys, values, d_out):
    block = jax.ShapeDtypeStruct((ROWS, HEADS * DIM), BF16)
    vmem = pl.BlockSpec(memory_space=pltpu.VMEM)
    dma = pltpu.SemaphoreType.DMA
    results = pl.pallas_call(
        kernel,
        out_shape=(block,) * 4,
        in_specs=[pl.BlockSpec(memory_space=pl.ANY)] * 4,
        out_specs=(vmem,) * 4,
        scratch_shapes=[
            pltpu.VMEM((HEADS, 3, 2, ROWS, DIM), BF16),
            pltpu.VMEM((HEADS, HOPS, 2, ROWS, DIM), BF16),
            pltpu.VMEM((LAG + 1, 3, ROWS, QUERIES), F32),
            pltpu.VMEM((LAG + 1, 3, ROWS, QUERIES), F32),
            pltpu.VMEM((3, ROWS, QUERIES), BF16),
            pltpu.VMEM((3, ROWS, QUERIES), BF16),
            pltpu.VMEM((LAG + 1, 3, 1, QUERIES), F32),
            pltpu.VMEM((HEADS, 2, QUERIES), F32),
            pltpu.VMEM((HEADS, 6, 2, QUERIES), F32),
            pltpu.VMEM((HEADS, 2, ROWS, DIM), F32),
            pltpu.VMEM((HEADS, 2, 2, ROWS, DIM), BF16),
            pltpu.VMEM((HEADS, 2, 2, ROWS, DIM), BF16),
            pltpu.VMEM((HEADS // 2, 2, ROWS, DIM), BF16),
            pltpu.VMEM((HEADS, HOPS, 2, ROWS, DIM), BF16),
            pltpu.VMEM((HEADS, HOPS - 1, 2, ROWS, DIM), BF16),
            pltpu.VMEM((HEADS, 2, ROWS, DIM), BF16),
            pltpu.VMEM((HEADS // 2, HOPS - 1, 2, ROWS, DIM), BF16),
            dma((HEADS, 4)),
            dma((HEADS, 2)), dma((HEADS, 2)), dma((HEADS // 2,)),
            dma((HEADS, 3)), dma((HEADS, 3)), dma((HEADS,)), dma((HEADS,)), dma((HEADS,)),
            dma((HEADS, 6)), dma((HEADS, 6)),
            dma((HEADS, 2)), dma((HEADS, 2)),
            dma((HEADS // 2,)), dma((HEADS // 2,)), dma((HEADS // 2,)),
            dma((HEADS, 3)), dma((HEADS, 3)),
            dma((HEADS // 2, 3)), dma((HEADS // 2, 3)),
        ],
        compiler_params=pltpu.CompilerParams(
            collective_id=0, has_side_effects=True, vmem_limit_bytes=56 << 20
        ),
        cost_estimate=pl.CostEstimate(
            flops=12 * HEADS * KEYS * QUERIES * DIM,
            bytes_accessed=8 * ROWS * HEADS * DIM * 2,
            transcendentals=HEADS * KEYS * QUERIES,
        ),
        name="window_attention",
    )(queries, keys, values, d_out)
    return pl.pallas_call(
        store,
        out_shape=(block,) * 4,
        in_specs=[vmem] * 4,
        out_specs=(vmem,) * 4,
        name="store_results",
    )(*results)


def solution(mesh):
    placed = P(("outer", "inner"), None)
    return jax.shard_map(
        on_device,
        mesh=mesh,
        in_specs=(placed,) * 4,
        out_specs=(placed,) * 4,
        check_vma=False,
    )
```
